32 devices in a mesh: ctx: 8 (over z, y), head: 4 (over x, core).
Axes of the slice: x: 2, y: 2, z: 4, core: 2. Of those that a mesh axis runs over, the one named last changes fastest.
Arguments:
- queries: bfloat16 [4096, 8192], P(('ctx', 'head')), may hold values from -7.5 to 7.5
- keys: bfloat16 [4096, 1024], P(('ctx', 'head')), may hold values from -6 to 6
- values: bfloat16 [4096, 1024], P(('ctx', 'head')), may hold values from -6 to 6
- out_grad: bfloat16 [4096, 8192], P(('ctx', 'head')), may hold values from -6 to 6
- segment_tiles: int32 [8], replicated, may hold values from 1 to 8, 32 in all
- parent_list: int32 [8], replicated, may hold values from 0 to 6, as said below
Outputs:
- attn_out: bfloat16 [4096, 8192], P(('ctx', 'head'))
- query_grad: bfloat16 [4096, 8192], P(('ctx', 'head'))
- key_grad: bfloat16 [4096, 1024], P(('ctx', 'head'))
- value_grad: bfloat16 [4096, 1024], P(('ctx', 'head'))
The draws below stay inside these ranges and needn't reach their ends.
Inputs may be any that keep to these rules, and one draw needn't show every extreme that they name: parent_list[0] is 0, the root; the parent of every other segment comes before it, and no segment lies more than 3 levels below the root.
All inputs are finite; a program needn't handle non-finite values.
Results may differ from the reference program's by a relative error of at most 0.017.
Values may be sent and summed in bfloat16 or wider, within the bound.
No kernel may reach another device: no remote copies, remote signals or barrier semaphores. Data moves between devices by JAX's collectives and lax.ppermute only.
A program may use at most 128 MiB of HBM per device.

```python
import math
import jax
import jax.numpy as jnp
import numpy as np
from jax import lax

QH = 64
KVH = 8
HD = 128
TILE = 128
MOST = 8
DEPTH = 3
TOK_DEV = 512
TOKENS = 4096
TILES = 32
SEGS = 8
N_CTX = 8


def draw_keys(key, part):
    key = jax.random.fold_in(key, 3)
    drawn = jnp.clip(jax.random.normal(key, (TOKENS, KVH, HD), jnp.float32), -6.0, 6.0)
    return drawn.reshape(TOKENS, KVH * HD).astype(jnp.bfloat16)


def draw_queries(key, part):
    key = jax.random.fold_in(key, 5)
    drawn = jnp.clip(jax.random.normal(key, (TOKENS, QH, HD), jnp.float32), -6.0, 6.0)
    return drawn.reshape(TOKENS, QH * HD).astype(jnp.bfloat16)


def draw_parent_list(key, part):
    key = jax.random.fold_in(key, 7)

    def place(segment, tables):
        parents, depths = tables
        candidate = jax.random.randint(jax.random.fold_in(key, segment), (), 0, segment).astype(jnp.int32)
        limit = jnp.where(segment == SEGS - 2, DEPTH - 1, DEPTH)
        candidate = jnp.where(depths[candidate] >= limit, parents[candidate], candidate)
        candidate = jnp.where(depths[candidate] >= limit, parents[candidate], candidate)
        candidate = jnp.where(depths[candidate] >= limit, parents[candidate], candidate)
        return (parents.at[segment].set(candidate), depths.at[segment].set(depths[candidate] + 1))
    start_tables = (jnp.zeros((SEGS,), jnp.int32), jnp.zeros((SEGS,), jnp.int32))
    parents, depths = lax.fori_loop(1, SEGS - 1, place, start_tables)
    parents = parents.at[SEGS - 1].set(SEGS - 2)
    return parents


def steps_of(own_key, shape, cuts, low, high):
    loudness = 1.0
    for dim, parts in cuts:
        steps = jax.random.uniform(jax.random.fold_in(jax.random.fold_in(own_key, 6), dim), (parts,), jnp.float32, low / len(cuts), high / len(cuts))
        loudness = loudness * jnp.repeat(jnp.exp(steps), shape[dim] // parts).reshape((-1,) + (1,) * (len(shape) - 1 - dim))
    return loudness


def split_up(amount, total, bound, slope):
    loads = [(1 << 20) // math.isqrt(standing ** slope) + 1 for standing in range(2, amount + 1)]
    surplus, given = total - bound - (amount - 1), [1] * (amount - 1)
    while surplus > 0:
        candidates = [i for i in range(amount - 1) if given[i] < bound]
        pool, left = sum([loads[i] for i in candidates]), surplus
        for i in candidates:
            extra = min(bound - given[i], max(1, left * loads[i] // pool), surplus)
            given[i] = given[i] + extra
            surplus = surplus - extra
    return np.array([bound] + given)


def ragged_sizes(rng, amount, total, bound, lean):
    if amount == 2:
        one = jax.random.randint(rng, (), max(1, total - bound), min(bound, total - 1) + 1)
        return jnp.stack([one, total - one])
    lengths = jnp.asarray(split_up(amount, total, bound, lean), jnp.int32)
    couples = (amount - 1) // 2
    giver, sink = lengths[1:1 + 2 * couples:2], lengths[2:2 + 2 * couples:2]
    slack = jnp.minimum(giver - 1, bound - sink)
    shifted = jax.random.randint(jax.random.fold_in(rng, 1), (couples,), 0, 1 << 20) % (slack + 1)
    lengths = lengths.at[1:1 + 2 * couples:2].set(giver - shifted).at[2:2 + 2 * couples:2].set(sink + shifted)
    return lengths[jax.random.permutation(jax.random.fold_in(rng, 2), amount)]


def normal_values(rng, dims, scale, bound, cuts=(), held_as=jnp.bfloat16):
    loudness = steps_of(rng, dims, cuts, -0.22, 0.18) if cuts else 1.0
    array = jax.random.normal(rng, dims, jnp.float32) * scale * loudness
    return jnp.minimum(jnp.maximum(array, -bound), bound).astype(held_as)


def setup_inputs(seed: int = 0) -> dict:
    arg_keys = jax.random.split(jax.random.key(seed), 7)
    queries = draw_queries(jax.random.fold_in(arg_keys[6], 71), 0)
    keys = draw_keys(jax.random.fold_in(arg_keys[6], 71), 0)
    values = normal_values(arg_keys[2], (TOKENS, KVH * HD), 1.0, 6.0, ((0, 32),))
    out_grad = normal_values(arg_keys[3], (TOKENS, QH * HD), 1.0, 6.0, ((0, 32),))
    segment_tiles = ragged_sizes(arg_keys[4], SEGS, TILES, MOST, 1).astype(jnp.int32)
    parent_list = draw_parent_list(jax.random.fold_in(arg_keys[6], 71), 0)
    return dict(queries=queries, keys=keys, values=values, out_grad=out_grad, segment_tiles=segment_tiles, parent_list=parent_list)


def ancestry(parent_list):
    count = parent_list.shape[0]
    numbers = jnp.arange(count, dtype=jnp.int32)
    parent_map = (parent_list[:, None] == numbers[None, :]).astype(jnp.float32)
    ancestor_map = jnp.maximum(parent_map, (numbers[:, None] == numbers[None, :]).astype(jnp.float32))
    for squaring in range(count.bit_length()):
        ancestor_map = (jnp.dot(ancestor_map, ancestor_map, preferred_element_type=jnp.float32) > 0.5).astype(jnp.float32)
    return ancestor_map

def segment_table(positions, segment_tiles, tile):
    segment_ends = jnp.cumsum(segment_tiles, dtype=jnp.int32) * tile
    segment = lax.optimization_barrier(jnp.sum((positions[:, None] >= segment_ends[None, :]).astype(jnp.int32), axis=1))
    numbers = jnp.arange(segment_tiles.shape[0], dtype=jnp.int32)
    return (segment[:, None] == numbers[None, :]).astype(jnp.float32)

def visible_pairs(query_reach, query_pos, key_pos, segment_tiles, tile):
    key_table = segment_table(key_pos, segment_tiles, tile)
    allowed = jnp.dot(query_reach, key_table.T, preferred_element_type=jnp.float32) > 0.5
    return allowed & (key_pos[None, :] <= query_pos[:, None])

def forward_tiles(running, key_piece, value_piece, first, query_block, query_reach, query_pos, segment_tiles, tile, scaling):
    groups = query_block.shape[1]
    width = query_block.shape[3]
    tile_count = key_piece.shape[0] // tile

    def one_tile(tile_index, status):
        offset = (tile_index * tile).astype(jnp.int32)
        key_tile = lax.dynamic_slice_in_dim(key_piece, offset, tile, 0).reshape(tile, groups, width)
        value_tile = lax.dynamic_slice_in_dim(value_piece, offset, tile, 0).reshape(tile, groups, width)
        key_pos = (first + offset).astype(jnp.int32) + jnp.arange(tile, dtype=jnp.int32)
        visible_map = visible_pairs(query_reach, query_pos, key_pos, segment_tiles, tile)

        def attend(inner):
            maximum, totals, accumulated = inner
            scores = jnp.einsum('qgrd,kgd->grqk', query_block, key_tile, preferred_element_type=jnp.float32) * scaling
            scores = jnp.where(visible_map[None, None], scores, -1e+30)
            new_max = jnp.maximum(maximum, lax.optimization_barrier(jnp.max(scores, axis=-1)))
            weights = jnp.where(visible_map[None, None], jnp.exp(scores - new_max[..., None]), 0.0)
            factor = jnp.exp(maximum - new_max)
            totals = factor * totals + lax.optimization_barrier(jnp.sum(weights, axis=-1))
            product = jnp.einsum('grqk,kgd->grqd', weights.astype(jnp.bfloat16), value_tile, preferred_element_type=jnp.float32)
            accumulated = factor[..., None] * accumulated + product
            return (new_max, totals, accumulated)

        def unchanged(inner):
            return inner
        return lax.cond(jnp.any(visible_map), attend, unchanged, status)
    return lax.fori_loop(0, tile_count, one_tile, running)

def backward_tiles(running, key_piece, value_piece, first, query_block, grad_block, log_totals, row_dots, query_reach, query_pos, segment_tiles, tile, scaling):
    groups = query_block.shape[1]
    width = query_block.shape[3]
    tile_count = key_piece.shape[0] // tile

    def one_tile(tile_index, status):
        offset = (tile_index * tile).astype(jnp.int32)
        key_tile = lax.dynamic_slice_in_dim(key_piece, offset, tile, 0).reshape(tile, groups, width)
        value_tile = lax.dynamic_slice_in_dim(value_piece, offset, tile, 0).reshape(tile, groups, width)
        key_pos = (first + offset).astype(jnp.int32) + jnp.arange(tile, dtype=jnp.int32)
        visible_map = visible_pairs(query_reach, query_pos, key_pos, segment_tiles, tile)

        def attend(inner):
            query_acc, key_acc, value_acc = inner
            scores = jnp.einsum('qgrd,kgd->grqk', query_block, key_tile, preferred_element_type=jnp.float32) * scaling
            scores = jnp.where(visible_map[None, None], scores, -1e+30)
            weights = jnp.where(visible_map[None, None], jnp.exp(scores - log_totals[..., None]), 0.0)
            value_term = jnp.einsum('grqk,qgrd->kgd', weights.astype(jnp.bfloat16), grad_block, preferred_element_type=jnp.float32)
            weight_grad = jnp.einsum('qgrd,kgd->grqk', grad_block, value_tile, preferred_element_type=jnp.float32)
            score_grad = (weights * (weight_grad - row_dots[..., None])).astype(jnp.bfloat16)
            query_acc = query_acc + jnp.einsum('grqk,kgd->qgrd', score_grad, key_tile, preferred_element_type=jnp.float32) * scaling
            key_term = jnp.einsum('grqk,qgrd->kgd', score_grad, query_block, preferred_element_type=jnp.float32) * scaling
            position = (first + offset).astype(jnp.int32)
            previous = lax.dynamic_slice_in_dim(key_acc, position, tile, 0)
            key_acc = lax.dynamic_update_slice_in_dim(key_acc, previous + key_term.reshape(tile, groups * width), position, 0)
            previous = lax.dynamic_slice_in_dim(value_acc, position, tile, 0)
            value_acc = lax.dynamic_update_slice_in_dim(value_acc, previous + value_term.reshape(tile, groups * width), position, 0)
            return (query_acc, key_acc, value_acc)

        def unchanged(inner):
            return inner
        return lax.cond(jnp.any(visible_map), attend, unchanged, status)
    return lax.fori_loop(0, tile_count, one_tile, running)

def reference(queries, keys, values, out_grad, segment_tiles, parent_list):
    token_count = queries.shape[0]
    per_group = QH // KVH
    scaling = 1.0 / math.sqrt(HD)
    ancestor_map = ancestry(parent_list)
    query_rows = queries.reshape(token_count, KVH, per_group, HD)
    grad_rows = out_grad.reshape(token_count, KVH, per_group, HD)

    def block(totals_in, block_index):
        key_total, value_total = totals_in
        first = (block_index * TOK_DEV).astype(jnp.int32)
        query_block = lax.dynamic_slice_in_dim(query_rows, first, TOK_DEV, 0)
        grad_block = lax.dynamic_slice_in_dim(grad_rows, first, TOK_DEV, 0)
        query_pos = first + jnp.arange(TOK_DEV, dtype=jnp.int32)
        query_reach = jnp.dot(segment_table(query_pos, segment_tiles, TILE), ancestor_map, preferred_element_type=jnp.float32)
        start_state = (jnp.full((KVH, per_group, TOK_DEV), -1e+30, jnp.float32), jnp.zeros((KVH, per_group, TOK_DEV), jnp.float32), jnp.zeros((KVH, per_group, TOK_DEV, HD), jnp.float32))
        maximum, sums, accumulated = forward_tiles(start_state, keys, values, jnp.int32(0), query_block, query_reach, query_pos, segment_tiles, TILE, scaling)
        attended = (accumulated / sums[..., None]).astype(jnp.bfloat16)
        attended_rows = attended.transpose(2, 0, 1, 3)
        log_totals = maximum + jnp.log(sums)
        row_dots = lax.optimization_barrier(jnp.sum(grad_block.astype(jnp.float32) * attended_rows.astype(jnp.float32), axis=-1)).transpose(1, 2, 0)
        back_state = (jnp.zeros((TOK_DEV, KVH, per_group, HD), jnp.float32), jnp.zeros((token_count, KVH * HD), jnp.float32), jnp.zeros((token_count, KVH * HD), jnp.float32))
        query_acc, key_acc, value_acc = backward_tiles(back_state, keys, values, jnp.int32(0), query_block, grad_block, log_totals, row_dots, query_reach, query_pos, segment_tiles, TILE, scaling)
        key_part = lax.optimization_barrier(key_acc.astype(jnp.bfloat16))
        value_part = lax.optimization_barrier(value_acc.astype(jnp.bfloat16))
        key_total = key_total + key_part.astype(jnp.float32)
        value_total = value_total + value_part.astype(jnp.float32)
        return ((key_total, value_total), (attended_rows.reshape(TOK_DEV, QH * HD), query_acc.astype(jnp.bfloat16).reshape(TOK_DEV, QH * HD)))
    zero_grads = (jnp.zeros((token_count, KVH * HD), jnp.float32), jnp.zeros((token_count, KVH * HD), jnp.float32))
    grads, outputs = lax.scan(block, zero_grads, jnp.arange(N_CTX, dtype=jnp.int32))
    attn_out = outputs[0].reshape(token_count, QH * HD)
    query_grad = outputs[1].reshape(token_count, QH * HD)
    return (attn_out, query_grad, grads[0].astype(jnp.bfloat16), grads[1].astype(jnp.bfloat16))
```

```python
import functools
import math

import jax
import jax.numpy as jnp
from jax import lax
from jax.experimental import pallas as pl
from jax.experimental.pallas import tpu as pltpu
from jax.sharding import PartitionSpec as P

HD = 128
TILE = 128
LEVELS = 4
MOST = 8
NEG = -1e30
SCALE = 1.0 / math.sqrt(HD)
LOG2E = 1.4426950408889634
bf16 = jnp.bfloat16
f32 = jnp.float32


def visible_lists(segment_tiles, parent_list, first, here, tiles, slot_of):
    count = segment_tiles.shape[0]
    ends = jnp.cumsum(segment_tiles, dtype=jnp.int32)
    numbers = jnp.arange(count, dtype=jnp.int32)
    key_tiles = jnp.arange(tiles, dtype=jnp.int32)
    key_seg = jnp.sum((key_tiles[:, None] >= ends[None, :]).astype(jnp.int32), axis=1)
    mine = first + jnp.arange(here, dtype=jnp.int32)
    seg = jnp.sum((mine[:, None] >= ends[None, :]).astype(jnp.int32), axis=1)
    seen = jnp.zeros((here, tiles), jnp.bool_)
    for level in range(LEVELS):
        seen = seen | (seg[:, None] == key_seg[None, :])
        seg = jnp.sum(jnp.where(seg[:, None] == numbers[None, :], parent_list[None, :], 0), axis=1)
    seen = seen & (key_tiles[None, :] <= mine[:, None])
    rank = jnp.cumsum(seen.astype(jnp.int32), axis=1) - 1
    most = min(tiles, LEVELS * MOST)
    places = jnp.arange(most, dtype=jnp.int32)
    chosen = seen[:, :, None] & (rank[:, :, None] == places[None, None, :])
    lists = jnp.sum(jnp.where(chosen, slot_of[None, :, None], 0), axis=1)
    return lists.astype(jnp.int32), jnp.sum(seen.astype(jnp.int32), axis=1)


def mm(a, b, ca=1, cb=0):
    return lax.dot_general(a, b, (((ca,), (cb,)), ((), ())), preferred_element_type=f32)


def attend_kernel(
    vis, cnt, q, do, k, v, o, dq, dkv, kt, vt, qt, dt, s_buf, p_buf, o_acc, q_acc, dka, dva, *, heads, last
):
    t = pl.program_id(1)
    part = pl.program_id(2)
    rows = heads * TILE
    tiles = k.shape[0]

    @pl.when((t == 0) & (part == 0))
    def _():
        def prepare(i, c):
            kt[i] = k[i].T
            vt[i] = v[i].T
            dka[i] = jnp.zeros((HD, TILE), f32)
            dva[i] = jnp.zeros((HD, TILE), f32)
            return c

        lax.fori_loop(0, tiles, prepare, 0)

    for h in range(heads):
        cols = pl.ds(h * HD, HD)
        qt[:, cols] = q[0, :, cols].T
        dt[:, cols] = do[0, :, cols].T
    n = cnt[t]
    blocks = (n + 1) // 2

    def pair(ref, b, axis):
        return jnp.concatenate([ref[vis[t, 2 * b]], ref[vis[t, 2 * b + 1]]], axis=axis)

    def scores(b, m8, masked):
        s = mm(pair(k, b, 0), qt[...])
        if masked:
            key = lax.broadcasted_iota(jnp.int32, (2 * TILE, rows), 0)
            token = lax.broadcasted_iota(jnp.int32, (2 * TILE, rows), 1) % TILE
            s = jnp.where(key <= token + (1 - n % 2) * TILE, s, NEG)
        s_buf[b] = s
        return jnp.maximum(m8, jnp.max(s.reshape(2 * TILE // 8, 8, rows), axis=0))

    m8 = jnp.full((8, rows), NEG, f32)
    m8 = lax.fori_loop(0, blocks - 1, lambda b, c: scores(b, c, False), m8)
    m8 = scores(blocks - 1, m8, True)
    m = jnp.max(m8, axis=0, keepdims=True)

    o_acc[...] = jnp.zeros_like(o_acc)

    def weigh(b, l8):
        p = jnp.exp2((s_buf[b] - m) * (SCALE * LOG2E))
        pb = p.astype(bf16)
        p_buf[b] = pb
        o_acc[...] += mm(pair(vt, b, 1), pb)
        return l8 + jnp.sum(p.reshape(2 * TILE // 8, 8, rows), axis=0)

    l8 = lax.fori_loop(0, blocks, weigh, jnp.zeros((8, rows), f32))
    inv = 1.0 / jnp.sum(l8, axis=0, keepdims=True)
    ob = (o_acc[...] * inv).astype(bf16)
    db = (dt[...].astype(f32) * inv).astype(bf16)
    dt[...] = db
    rowdot = jnp.sum(db.astype(f32) * ob.astype(f32), axis=0, keepdims=True)
    for h in range(heads):
        cols = slice(h * HD, (h + 1) * HD)
        o[0, :, cols] = ob[:, cols].T

    q_acc[...] = jnp.zeros_like(q_acc)

    def back(b, c):
        pb = p_buf[b]
        dp = mm(pair(v, b, 0), dt[...])
        ds = (pb.astype(f32) * (dp - rowdot)).astype(bf16)
        dvt = mm(dt[...], pb, 1, 1)
        dkt = mm(qt[...], ds, 1, 1)
        q_acc[...] += mm(pair(kt, b, 1), ds)
        one = vis[t, 2 * b]
        two = vis[t, 2 * b + 1]
        dva[one] += dvt[:, :TILE]
        dva[two] += dvt[:, TILE:]
        dka[one] += dkt[:, :TILE]
        dka[two] += dkt[:, TILE:]
        return c

    lax.fori_loop(0, blocks, back, 0)
    qb = (q_acc[...] * SCALE).astype(bf16)
    for h in range(heads):
        cols = slice(h * HD, (h + 1) * HD)
        dq[0, :, cols] = qb[:, cols].T

    @pl.when((t == last[0]) & (part == last[1]))
    def _():
        def finish(i, c):
            dkv[i, :, :HD] = (dka[i] * SCALE).astype(bf16).T
            dkv[i, :, HD:] = dva[i].astype(bf16).T
            return c

        lax.fori_loop(0, tiles, finish, 0)


def attend(vis, cnt, q, do, kv, heads):
    here, _, width = q.shape
    tiles = kv.shape[0]
    groups = width // (heads * TILE)
    most = vis.shape[1]
    parts = 1 if tiles <= 64 else 2
    heads = heads // parts
    rows = heads * TILE
    rowspec = pl.BlockSpec((1, TILE, rows), lambda g, t, p, *_: (t, 0, g * parts + p))
    keyspec = pl.BlockSpec((tiles, TILE, HD), lambda g, t, p, *_: (0, 0, 2 * g), pipeline_mode=pl.Buffered(1))
    valspec = pl.BlockSpec((tiles, TILE, HD), lambda g, t, p, *_: (0, 0, 2 * g + 1), pipeline_mode=pl.Buffered(1))
    gradspec = pl.BlockSpec((tiles, TILE, 2 * HD), lambda g, t, p, *_: (0, 0, g), pipeline_mode=pl.Buffered(1))
    return pl.pallas_call(
        functools.partial(attend_kernel, heads=heads, last=(here - 1, parts - 1)),
        grid_spec=pltpu.PrefetchScalarGridSpec(
            num_scalar_prefetch=2,
            grid=(groups, here, parts),
            in_specs=[rowspec, rowspec, keyspec, valspec],
            out_specs=[rowspec, rowspec, gradspec],
            scratch_shapes=[
                pltpu.VMEM((tiles, HD, TILE), bf16),
                pltpu.VMEM((tiles, HD, TILE), bf16),
                pltpu.VMEM((HD, rows), bf16),
                pltpu.VMEM((HD, rows), bf16),
                pltpu.VMEM((most // 2, 2 * TILE, rows), f32),
                pltpu.VMEM((most // 2, 2 * TILE, rows), bf16),
                pltpu.VMEM((HD, rows), f32),
                pltpu.VMEM((HD, rows), f32),
                pltpu.VMEM((tiles, HD, TILE), f32),
                pltpu.VMEM((tiles, HD, TILE), f32),
            ],
        ),
        out_shape=[
            jax.ShapeDtypeStruct((here, TILE, width), bf16),
            jax.ShapeDtypeStruct((here, TILE, width), bf16),
            jax.ShapeDtypeStruct((tiles, TILE, 2 * HD * groups), bf16),
        ],
        compiler_params=pltpu.CompilerParams(vmem_limit_bytes=63 << 20),
        cost_estimate=pl.CostEstimate(flops=40_000_000_000, bytes_accessed=20_000_000, transcendentals=20_000_000),
        name="attend",
    )(vis, cnt, q, do, kv, kv)


def snake(z_size, y_size):
    order = [z * y_size for z in range(z_size)]
    for z in reversed(range(z_size)):
        across = range(1, y_size)
        order += [z * y_size + y for y in (across if (z_size - 1 - z) % 2 == 0 else reversed(across))]
    return order


def ring_gather(block, forth, back, size):
    up = down = block
    got = [block]
    for step in range(size // 2 - 1):
        up = lax.ppermute(up, "ctx", forth)
        down = lax.ppermute(down, "ctx", back)
        got += [up, down]
    half = block.shape[-1] // 2
    up = lax.ppermute(up[..., :half], "ctx", forth)
    down = lax.ppermute(down[..., half:], "ctx", back)
    return got + [jnp.concatenate([up, down], axis=-1)]


def ring_sum(parts, forth, back, size):
    half = parts[0].shape[-1] // 2
    far = parts[size - 1]
    up, down = lax.ppermute(far[..., :half], "ctx", back), lax.ppermute(far[..., half:], "ctx", forth)

    def add(a, b):
        return (a.astype(f32) + b.astype(f32)).astype(bf16)

    for step in reversed(range(size // 2 - 1)):
        mine_up, mine_down = parts[1 + 2 * step], parts[2 + 2 * step]
        if step == size // 2 - 2:
            up = jnp.concatenate([add(mine_up[..., :half], up), mine_up[..., half:]], axis=-1)
            down = jnp.concatenate([mine_down[..., :half], add(mine_down[..., half:], down)], axis=-1)
        else:
            up, down = add(mine_up, up), add(mine_down, down)
        up, down = lax.ppermute(up, "ctx", back), lax.ppermute(down, "ctx", forth)
    return (parts[0].astype(f32) + up.astype(f32) + down.astype(f32)).astype(bf16)


def local(queries, keys, values, out_grad, segment_tiles, parent_list):
    rows_here, key_width = keys.shape
    ctx, heads_axis = lax.axis_size("ctx"), lax.axis_size("head")
    groups = key_width // HD // heads_axis
    heads = queries.shape[1] // key_width
    tiles = ctx * heads_axis * rows_here // TILE
    here = tiles // ctx

    y_size = heads_axis // 2
    order = snake(ctx // y_size, y_size)
    forth = [(order[i], order[(i + 1) % ctx]) for i in range(ctx)]
    back = [(b, a) for a, b in forth]
    place = [order.index(c) for c in range(ctx)]
    piece_of = [0] * ctx
    for d in range(1, ctx):
        piece_of[d] = 2 * d - 1 if d <= ctx // 2 else 2 * (ctx - d)
    me = lax.axis_index("ctx")
    places = jnp.asarray(place, jnp.int32)
    my_place = jnp.sum(jnp.where(jnp.arange(ctx) == me, places, 0))
    distance = jnp.repeat(jnp.mod(my_place - places, ctx), here)
    table = jnp.asarray(piece_of, jnp.int32)
    piece = jnp.sum(jnp.where(distance[:, None] == jnp.arange(ctx)[None, :], table[None, :], 0), axis=1)
    slot_of = piece * here + jnp.arange(tiles, dtype=jnp.int32) % here
    vis, cnt = visible_lists(segment_tiles, parent_list, me * here, here, tiles, slot_of)

    def swap(x):
        return lax.all_to_all(x, "head", split_axis=0, concat_axis=0, tiled=True)

    def to_heads(x):
        x = x.reshape(rows_here, heads_axis, -1).transpose(1, 0, 2)
        return swap(x).reshape(here, TILE, -1)

    def to_tokens(x):
        return swap(x.reshape(heads_axis, rows_here, -1)).transpose(1, 0, 2)

    kv = jnp.concatenate(
        [keys.reshape(rows_here, heads_axis, groups, HD), values.reshape(rows_here, heads_axis, groups, HD)], axis=3
    )
    kv = to_heads(kv)
    kv = jnp.concatenate(ring_gather(kv, forth, back, ctx), axis=0)
    q = to_heads(queries)
    do = to_heads(out_grad)

    o, dq, dkv = attend(vis, cnt, q, do, kv, heads)

    o = to_tokens(o).reshape(queries.shape)
    dq = to_tokens(dq).reshape(queries.shape)
    dkv = ring_sum([dkv[i * here : (i + 1) * here] for i in range(ctx)], forth, back, ctx)
    dkv = to_tokens(dkv).reshape(rows_here, heads_axis, groups, 2, HD)
    dk = dkv[:, :, :, 0].reshape(keys.shape)
    dv = dkv[:, :, :, 1].reshape(values.shape)
    return o, dq, dk, dv


def solution(mesh):
    rows = P(("ctx", "head"), None)
    return jax.shard_map(
        local,
        mesh=mesh,
        in_specs=(rows, rows, rows, rows, P(), P()),
        out_specs=(rows, rows, rows, rows),
        check_vma=False,
    )
```

```python
import functools
import math

import jax
import jax.numpy as jnp
from jax import lax
from jax.experimental import pallas as pl
from jax.experimental.pallas import tpu as pltpu
from jax.sharding import PartitionSpec as P

HD = 128
TILE = 128
LEVELS = 4
MOST = 8
WIDE = 4
NEG = -1e30
SCALE = 1.0 / math.sqrt(HD)
LOG2E = 1.4426950408889634
bf16 = jnp.bfloat16
f32 = jnp.float32


def visible_lists(segment_tiles, parent_list, first, here, tiles, slot_of):
    count = segment_tiles.shape[0]
    ends = jnp.cumsum(segment_tiles, dtype=jnp.int32)
    numbers = jnp.arange(count, dtype=jnp.int32)
    key_tiles = jnp.arange(tiles, dtype=jnp.int32)
    key_seg = jnp.sum((key_tiles[:, None] >= ends[None, :]).astype(jnp.int32), axis=1)
    mine = first + jnp.arange(here, dtype=jnp.int32)
    seg = jnp.sum((mine[:, None] >= ends[None, :]).astype(jnp.int32), axis=1)
    seen = jnp.zeros((here, tiles), jnp.bool_)
    for level in range(LEVELS):
        seen = seen | (seg[:, None] == key_seg[None, :])
        seg = jnp.sum(jnp.where(seg[:, None] == numbers[None, :], parent_list[None, :], 0), axis=1)
    seen = seen & (key_tiles[None, :] <= mine[:, None])
    rank = jnp.cumsum(seen.astype(jnp.int32), axis=1) - 1
    most = min(tiles, LEVELS * MOST)
    places = jnp.arange(most, dtype=jnp.int32)
    chosen = seen[:, :, None] & (rank[:, :, None] == places[None, None, :])
    slots = jnp.sum(jnp.where(chosen, slot_of[None, :, None], 0), axis=1)
    numbers = jnp.sum(jnp.where(chosen, key_tiles[None, :, None], 0), axis=1)
    return slots, numbers, jnp.sum(seen.astype(jnp.int32), axis=1)


def mm(a, b, ca=1, cb=0):
    return lax.dot_general(a, b, (((ca,), (cb,)), ((), ())), preferred_element_type=f32)


def attend_kernel(
    vis, into, cnt, qdo, k, v, odq, dkv, qt, dt, qn, dn, s_buf, p_buf, o_acc, q_acc, dka, dva, *, heads, last
):
    t = pl.program_id(0)
    part = pl.program_id(1)
    rows = heads * TILE

    @pl.when((t == 0) & (part == 0))
    def _():
        dka[...] = jnp.zeros_like(dka)
        dva[...] = jnp.zeros_like(dva)

    for h in range(heads):
        cols = slice(h * HD, (h + 1) * HD)
        qt[:, cols] = qdo[0, :, cols].T
        dt[:, cols] = qdo[0, :, rows + h * HD : rows + (h + 1) * HD].T
        qn[cols, :] = qdo[0, :, cols]
    n = cnt[t]
    full = (n - 1) // WIDE
    rest = n - full * WIDE

    def gathered(ref, b, wide):
        return jnp.concatenate([ref[vis[t, WIDE * b + w]] for w in range(wide)], axis=0)

    def over_blocks(step, start, first=None):
        carry = lax.fori_loop(0, full, lambda b, c: step(b, WIDE, False, c), start)
        return lax.cond(
            rest <= WIDE // 2,
            lambda c: step(full, WIDE // 2, True, c),
            lambda c: step(full, WIDE, True, c),
            carry,
        )

    def scores(b, wide, masked, m8):
        s = mm(gathered(k, b, wide), qt[...])
        if masked:
            key = lax.broadcasted_iota(jnp.int32, (wide * TILE, rows), 0)
            token = lax.broadcasted_iota(jnp.int32, (wide * TILE, rows), 1) % TILE
            s = jnp.where(key <= token + (rest - 1) * TILE, s, NEG)
        s_buf[b, : wide * TILE] = s
        return jnp.maximum(m8, jnp.max(s.reshape(wide * TILE // 8, 8, rows), axis=0))

    m8 = over_blocks(scores, jnp.full((8, rows), NEG, f32))
    m = jnp.max(m8, axis=0, keepdims=True)

    o_acc[...] = jnp.zeros_like(o_acc)

    def weigh(b, wide, masked, l8):
        p = jnp.exp2((s_buf[b, : wide * TILE] - m) * (SCALE * LOG2E))
        pb = p.astype(bf16)
        p_buf[b, : wide * TILE] = pb
        o_acc[...] += mm(gathered(v, b, wide), pb, 0, 0)
        return l8 + jnp.sum(p.reshape(wide * TILE // 8, 8, rows), axis=0)

    l8 = over_blocks(weigh, jnp.zeros((8, rows), f32))
    inv = 1.0 / jnp.sum(l8, axis=0, keepdims=True)
    ob = (o_acc[...] * inv).astype(bf16)
    db = (dt[...].astype(f32) * inv).astype(bf16)
    dt[...] = db
    rowdot = jnp.sum(db.astype(f32) * ob.astype(f32), axis=0, keepdims=True)
    for h in range(heads):
        cols = slice(h * HD, (h + 1) * HD)
        odq[0, :, cols] = ob[:, cols].T
        dn[cols, :] = db[:, cols].T

    q_acc[...] = jnp.zeros_like(q_acc)

    def back(b, wide, masked, carry):
        pb = p_buf[b, : wide * TILE]
        dp = mm(gathered(v, b, wide), dt[...])
        ds = (pb.astype(f32) * (dp - rowdot)).astype(bf16)
        dvn = mm(pb, dn[...])
        dkn = mm(ds, qn[...])
        q_acc[...] += mm(gathered(k, b, wide), ds, 0, 0)
        for w in range(wide):
            slot = into[t, WIDE * b + w]
            part_rows = slice(w * TILE, (w + 1) * TILE)
            dva[slot] += dvn[part_rows]
            dka[slot] += dkn[part_rows]
        return carry

    over_blocks(back, 0)
    qb = (q_acc[...] * SCALE).astype(bf16)
    for h in range(heads):
        odq[0, :, rows + h * HD : rows + (h + 1) * HD] = qb[:, h * HD : (h + 1) * HD].T

    @pl.when((t == last[0]) & (part == last[1]))
    def _():
        dkv[:, :, :HD] = (dka[...] * SCALE).astype(bf16)
        dkv[:, :, HD:] = dva[...].astype(bf16)


def parts_of(tiles):
    return 1 if tiles <= 64 else 2


def attend(vis, into, cnt, qdo, kv, number):
    here, _, width = qdo.shape
    tiles = kv.shape[0]
    most = vis.shape[1]
    parts = parts_of(tiles)
    rows = width // (2 * parts)
    rowspec = pl.BlockSpec((1, TILE, 2 * rows), lambda t, p, *_: (t, 0, p))
    keyspec = pl.BlockSpec((tiles, TILE, HD), lambda t, p, *_: (0, 0, 0), pipeline_mode=pl.Buffered(1))
    valspec = pl.BlockSpec((tiles, TILE, HD), lambda t, p, *_: (0, 0, 1), pipeline_mode=pl.Buffered(1))
    gradspec = pl.BlockSpec((tiles, TILE, 2 * HD), lambda t, p, *_: (0, 0, 0), pipeline_mode=pl.Buffered(1))
    return pl.pallas_call(
        functools.partial(attend_kernel, heads=rows // HD, last=(here - 1, parts - 1)),
        grid_spec=pltpu.PrefetchScalarGridSpec(
            num_scalar_prefetch=3,
            grid=(here, parts),
            in_specs=[rowspec, keyspec, valspec],
            out_specs=[rowspec, gradspec],
            scratch_shapes=[
                pltpu.VMEM((HD, rows), bf16),
                pltpu.VMEM((HD, rows), bf16),
                pltpu.VMEM((rows, HD), bf16),
                pltpu.VMEM((rows, HD), bf16),
                pltpu.VMEM((most // WIDE, WIDE * TILE, rows), f32),
                pltpu.VMEM((most // WIDE, WIDE * TILE, rows), bf16),
                pltpu.VMEM((HD, rows), f32),
                pltpu.VMEM((HD, rows), f32),
                pltpu.VMEM((tiles, TILE, HD), f32),
                pltpu.VMEM((tiles, TILE, HD), f32),
            ],
        ),
        out_shape=[
            jax.ShapeDtypeStruct((here, TILE, width), bf16),
            jax.ShapeDtypeStruct((tiles, TILE, 2 * HD), bf16),
        ],
        compiler_params=pltpu.CompilerParams(vmem_limit_bytes=63 << 20),
        cost_estimate=pl.CostEstimate(flops=40_000_000_000, bytes_accessed=20_000_000, transcendentals=20_000_000),
        name=f"attend{number}",
    )(vis, into, cnt, qdo, kv, kv)


def snake(z_size, y_size):
    order = [z * y_size for z in range(z_size)]
    for z in reversed(range(z_size)):
        across = range(1, y_size)
        order += [z * y_size + y for y in (across if (z_size - 1 - z) % 2 == 0 else reversed(across))]
    return order


def ring_gather(block, forth, back, size):
    up = down = block
    got = [block]
    for step in range(size // 2 - 1):
        up = lax.ppermute(up, "ctx", forth)
        down = lax.ppermute(down, "ctx", back)
        got += [up, down]
    half = block.shape[-1] // 2
    up = lax.ppermute(up[..., :half], "ctx", forth)
    down = lax.ppermute(down[..., half:], "ctx", back)
    return got + [jnp.concatenate([up, down], axis=-1)]


def ring_sum(parts, forth, back, size):
    half = parts[0].shape[-1] // 2
    far = parts[size - 1]
    up, down = lax.ppermute(far[..., :half], "ctx", back), lax.ppermute(far[..., half:], "ctx", forth)

    def add(a, b):
        return (a.astype(f32) + b.astype(f32)).astype(bf16)

    for step in reversed(range(size // 2 - 1)):
        mine_up, mine_down = parts[1 + 2 * step], parts[2 + 2 * step]
        if step == size // 2 - 2:
            up = jnp.concatenate([add(mine_up[..., :half], up), mine_up[..., half:]], axis=-1)
            down = jnp.concatenate([mine_down[..., :half], add(mine_down[..., half:], down)], axis=-1)
        else:
            up, down = add(mine_up, up), add(mine_down, down)
        up, down = lax.ppermute(up, "ctx", back), lax.ppermute(down, "ctx", forth)
    return (parts[0].astype(f32) + up.astype(f32) + down.astype(f32)).astype(bf16)


def local(queries, keys, values, out_grad, segment_tiles, parent_list):
    rows_here, key_width = keys.shape
    ctx, heads_axis = lax.axis_size("ctx"), lax.axis_size("head")
    groups = key_width // HD // heads_axis
    heads = queries.shape[1] // key_width
    tiles = ctx * heads_axis * rows_here // TILE
    here = tiles // ctx

    y_size = heads_axis // 2
    order = snake(ctx // y_size, y_size)
    forth = [(order[i], order[(i + 1) % ctx]) for i in range(ctx)]
    back = [(b, a) for a, b in forth]
    place = [order.index(c) for c in range(ctx)]
    piece_of = [0] * ctx
    for d in range(1, ctx):
        piece_of[d] = 2 * d - 1 if d <= ctx // 2 else 2 * (ctx - d)
    me = lax.axis_index("ctx")
    places = jnp.asarray(place, jnp.int32)
    my_place = jnp.sum(jnp.where(jnp.arange(ctx) == me, places, 0))
    distance = jnp.repeat(jnp.mod(my_place - places, ctx), here)
    table = jnp.asarray(piece_of, jnp.int32)
    piece = jnp.sum(jnp.where(distance[:, None] == jnp.arange(ctx)[None, :], table[None, :], 0), axis=1)
    slot_of = piece * here + jnp.arange(tiles, dtype=jnp.int32) % here
    slots, numbers, cnt = visible_lists(segment_tiles, parent_list, me * here, here, tiles, slot_of)

    def swap(x):
        return lax.all_to_all(x, "head", split_axis=0, concat_axis=0, tiled=True)

    def columns(x, number, width):
        return x[:, number * width : (number + 1) * width]

    parts = parts_of(tiles)
    width = heads * HD // parts

    def pair_of_rows(g):
        return jnp.stack(
            [
                jnp.concatenate(
                    [columns(x, (h * groups + g) * parts + p, width) for p in range(parts) for x in (queries, out_grad)],
                    axis=1,
                )
                for h in range(heads_axis)
            ]
        )

    def joined(pieces, which):
        w = pieces[0].shape[2] // (2 * parts)
        return jnp.concatenate(
            [
                columns(pieces[g][h], 2 * p + which, w)
                for h in range(heads_axis)
                for g in range(groups)
                for p in range(parts)
            ],
            axis=1,
        )

    kv = jnp.stack(
        [
            jnp.concatenate([columns(x, h * groups + g, HD) for g in range(groups) for x in (keys, values)], axis=1)
            for h in range(heads_axis)
        ]
    )
    qdo = [pair_of_rows(g) for g in range(groups)]
    kv = swap(kv).reshape(here, TILE, groups * 2 * HD)
    crossed = []
    for g in range(groups):
        qdo[g], before = lax.optimization_barrier((qdo[g], crossed[g - 1] if g else kv))
        if g:
            crossed[g - 1] = before
        else:
            kv = before
        crossed.append(swap(qdo[g]).reshape(here, TILE, -1))

    odq, dkv = [], []
    for g in range(groups):
        mine = kv[:, :, g * 2 * HD : (g + 1) * 2 * HD]
        if g == 0:
            ring = ring_gather(mine, forth, back, ctx)
            around, vis = jnp.concatenate(ring, axis=0), slots
        else:
            mine, ring[-1] = lax.optimization_barrier((mine, ring[-1]))
            around, vis = lax.all_gather(mine, "ctx", axis=0, tiled=True), numbers
        into = slots if g == groups - 1 else numbers
        odq_g, dkv_g = attend(vis, into, cnt, crossed[g], around, g)
        if g == groups - 1:
            if g:
                dkv_g, dkv[0] = lax.optimization_barrier((dkv_g, dkv[0]))
            dkv_g = ring_sum([dkv_g[i * here : (i + 1) * here] for i in range(ctx)], forth, back, ctx)
        else:
            dkv_g = lax.psum_scatter(dkv_g, "ctx", scatter_dimension=0, tiled=True)
        odq.append(swap(odq_g.reshape(heads_axis, rows_here, -1)))
        dkv.append(dkv_g)
    dkv = swap(jnp.concatenate(dkv, axis=-1).reshape(heads_axis, rows_here, -1))
    dk, dv = [
        jnp.concatenate(
            [columns(dkv[h], 2 * g + which, HD) for h in range(heads_axis) for g in range(groups)], axis=1
        )
        for which in range(2)
    ]
    return joined(odq, 0), joined(odq, 1), dk, dv


def solution(mesh):
    rows = P(("ctx", "head"), None)
    return jax.shard_map(
        local,
        mesh=mesh,
        in_specs=(rows, rows, rows, rows, P(), P()),
        out_specs=(rows, rows, rows, rows),
        check_vma=False,
    )
```

```python
import functools
import math

import jax
import jax.numpy as jnp
from jax import lax
from jax.experimental import pallas as pl
from jax.experimental.pallas import tpu as pltpu
from jax.sharding import PartitionSpec as P

HD = 128
TILE = 128
LEVELS = 4
MOST = 8
WIDE = 8
HALF = WIDE // 2
NEG = -1e30
SCALE = 1.0 / math.sqrt(HD)
LOG2E = 1.4426950408889634
bf16 = jnp.bfloat16
f32 = jnp.float32


def visible_lists(segment_tiles, parent_list, first, here, tiles):
    count = segment_tiles.shape[0]
    ends = jnp.cumsum(segment_tiles, dtype=jnp.int32)
    numbers = jnp.arange(count, dtype=jnp.int32)
    key_tiles = jnp.arange(tiles, dtype=jnp.int32)
    key_seg = jnp.sum((key_tiles[:, None] >= ends[None, :]).astype(jnp.int32), axis=1)
    mine = first + jnp.arange(here, dtype=jnp.int32)
    seg = jnp.sum((mine[:, None] >= ends[None, :]).astype(jnp.int32), axis=1)
    seen = jnp.zeros((here, tiles), jnp.bool_)
    for level in range(LEVELS):
        seen = seen | (seg[:, None] == key_seg[None, :])
        seg = jnp.sum(jnp.where(seg[:, None] == numbers[None, :], parent_list[None, :], 0), axis=1)
    seen = seen & (key_tiles[None, :] <= mine[:, None])
    rank = jnp.cumsum(seen.astype(jnp.int32), axis=1) - 1
    most = min(tiles, LEVELS * MOST)
    places = jnp.arange(most, dtype=jnp.int32)
    chosen = seen[:, :, None] & (rank[:, :, None] == places[None, None, :])
    numbers = jnp.sum(jnp.where(chosen, key_tiles[None, :, None], 0), axis=1)
    return numbers, jnp.sum(seen.astype(jnp.int32), axis=1)


def renamed(numbers, table):
    places = jnp.arange(table.shape[0], dtype=jnp.int32)
    return jnp.sum(jnp.where(numbers[:, :, None] == places, table, 0), axis=2)


def mm(a, b, ca=1, cb=0):
    return lax.dot_general(a, b, (((ca,), (cb,)), ((), ())), preferred_element_type=f32)


def attend_kernel(
    vis, into, cnt, qdo, k, v, odq, dkv, qt, dt, qn, dn, s_buf, p_buf, o_acc, q_acc, dka, dva, *, heads, last
):
    t = pl.program_id(0)
    part = pl.program_id(1)
    rows = heads * TILE

    @pl.when((t == 0) & (part == 0))
    def _():
        dka[...] = jnp.zeros_like(dka)
        dva[...] = jnp.zeros_like(dva)

    for h in range(heads):
        cols = slice(h * HD, (h + 1) * HD)
        qt[:, cols] = qdo[0, :, cols].T
        dt[:, cols] = qdo[0, :, rows + h * HD : rows + (h + 1) * HD].T
        qn[cols, :] = qdo[0, :, cols]
    n = cnt[t]
    wides = (n - 1) // WIDE
    halves = (n - 1) // HALF
    rest = n - halves * HALF

    def gathered(ref, at, wide):
        return jnp.concatenate([ref[vis[t, at + w]] for w in range(wide)], axis=0)

    def rows_of(at, wide):
        return pl.ds(pl.multiple_of(at * TILE, TILE), wide * TILE)

    def over_blocks(step, carry):
        carry = lax.fori_loop(0, wides, lambda b, c: step(b * WIDE, WIDE, False, c), carry)
        carry = lax.cond(
            halves > 2 * wides, lambda c: step(wides * WIDE, HALF, False, c), lambda c: c, carry
        )
        return lax.cond(
            rest <= HALF // 2,
            lambda c: step(halves * HALF, HALF // 2, True, c),
            lambda c: step(halves * HALF, HALF, True, c),
            carry,
        )

    def scores(at, wide, masked, m8):
        s = mm(gathered(k, at, wide), qt[...])
        if masked:
            key = lax.broadcasted_iota(jnp.int32, (wide * TILE, rows), 0)
            token = lax.broadcasted_iota(jnp.int32, (wide * TILE, rows), 1) % TILE
            s = jnp.where(key <= token + (rest - 1) * TILE, s, NEG)
        s_buf[rows_of(at, wide)] = s
        return jnp.maximum(m8, jnp.max(s.reshape(wide * TILE // 8, 8, rows), axis=0))

    m8 = over_blocks(scores, jnp.full((8, rows), NEG, f32))
    m = jnp.max(m8, axis=0, keepdims=True)

    o_acc[...] = jnp.zeros_like(o_acc)

    def weigh(at, wide, masked, l8):
        vb = gathered(v, at, wide)
        p = jnp.exp2((s_buf[rows_of(at, wide)] - m) * (SCALE * LOG2E))
        dp = mm(vb, dt[...])
        pb = p.astype(bf16)
        p_buf[rows_of(at, wide)] = pb
        s_buf[rows_of(at, wide)] = dp
        o_acc[...] += mm(vb, pb, 0, 0)
        return l8 + jnp.sum(p.reshape(wide * TILE // 8, 8, rows), axis=0)

    l8 = over_blocks(weigh, jnp.zeros((8, rows), f32))
    inv = 1.0 / jnp.sum(l8, axis=0, keepdims=True)
    ob = (o_acc[...] * inv).astype(bf16)
    grads = dt[...].astype(f32)
    db = (grads * inv).astype(bf16)
    rowdot = jnp.sum(grads * ob.astype(f32), axis=0, keepdims=True) * inv
    for h in range(heads):
        cols = slice(h * HD, (h + 1) * HD)
        odq[0, :, cols] = ob[:, cols].T
        dn[cols, :] = db[:, cols].T

    q_acc[...] = jnp.zeros_like(q_acc)

    def back(at, wide, masked, carry):
        pb = p_buf[rows_of(at, wide)]
        dp = s_buf[rows_of(at, wide)]
        ds = (pb.astype(f32) * (dp * inv - rowdot)).astype(bf16)
        dvn = mm(pb, dn[...])
        dkn = mm(ds, qn[...])
        q_acc[...] += mm(gathered(k, at, wide), ds, 0, 0)
        for w in range(wide):
            slot = into[t, at + w]
            part_rows = slice(w * TILE, (w + 1) * TILE)
            dva[slot] += dvn[part_rows]
            dka[slot] += dkn[part_rows]
        return carry

    over_blocks(back, 0)
    qb = (q_acc[...] * SCALE).astype(bf16)
    for h in range(heads):
        odq[0, :, rows + h * HD : rows + (h + 1) * HD] = qb[:, h * HD : (h + 1) * HD].T

    @pl.when((t == last[0]) & (part == last[1]))
    def _():
        dkv[:, :, :HD] = (dka[...] * SCALE).astype(bf16)
        dkv[:, :, HD:] = dva[...].astype(bf16)


def parts_of(tiles):
    return 1 if tiles <= 64 else 2


def attend(vis, into, cnt, qdo, kv, number):
    here, _, width = qdo.shape
    tiles = kv.shape[0]
    most = vis.shape[1]
    parts = parts_of(tiles)
    rows = width // (2 * parts)
    rowspec = pl.BlockSpec((1, TILE, 2 * rows), lambda t, p, *_: (t, 0, p))
    keyspec = pl.BlockSpec((tiles, TILE, HD), lambda t, p, *_: (0, 0, 0), pipeline_mode=pl.Buffered(1))
    valspec = pl.BlockSpec((tiles, TILE, HD), lambda t, p, *_: (0, 0, 1), pipeline_mode=pl.Buffered(1))
    gradspec = pl.BlockSpec((tiles, TILE, 2 * HD), lambda t, p, *_: (0, 0, 0), pipeline_mode=pl.Buffered(1))
    return pl.pallas_call(
        functools.partial(attend_kernel, heads=rows // HD, last=(here - 1, parts - 1)),
        grid_spec=pltpu.PrefetchScalarGridSpec(
            num_scalar_prefetch=3,
            grid=(here, parts),
            in_specs=[rowspec, keyspec, valspec],
            out_specs=[rowspec, gradspec],
            scratch_shapes=[
                pltpu.VMEM((HD, rows), bf16),
                pltpu.VMEM((HD, rows), bf16),
                pltpu.VMEM((rows, HD), bf16),
                pltpu.VMEM((rows, HD), bf16),
                pltpu.VMEM((most * TILE, rows), f32),
                pltpu.VMEM((most * TILE, rows), bf16),
                pltpu.VMEM((HD, rows), f32),
                pltpu.VMEM((HD, rows), f32),
                pltpu.VMEM((tiles, TILE, HD), f32),
                pltpu.VMEM((tiles, TILE, HD), f32),
            ],
        ),
        out_shape=[
            jax.ShapeDtypeStruct((here, TILE, width), bf16),
            jax.ShapeDtypeStruct((tiles, TILE, 2 * HD), bf16),
        ],
        compiler_params=pltpu.CompilerParams(vmem_limit_bytes=63 << 20),
        cost_estimate=pl.CostEstimate(flops=40_000_000_000, bytes_accessed=20_000_000, transcendentals=20_000_000),
        name=f"attend{number}",
    )(vis, into, cnt, qdo, kv, kv)


def snake(z_size, y_size):
    order = [z * y_size for z in range(z_size)]
    for z in reversed(range(z_size)):
        across = range(1, y_size)
        order += [z * y_size + y for y in (across if (z_size - 1 - z) % 2 == 0 else reversed(across))]
    return order


class Ring:
    def __init__(self, ctx, size, y_size):
        order = snake(size // y_size, y_size)
        self.size = size
        self.place = [order.index(c) for c in range(size)]
        self.forth = [
            (at + order[i], at + order[(i + 1) % size]) for at in range(0, ctx, size) for i in range(size)
        ]
        self.back = [(b, a) for a, b in self.forth]

    def piece(self, me, owner):
        places = jnp.asarray(self.place, jnp.int32)
        numbers = jnp.arange(self.size, dtype=jnp.int32)

        def place(c):
            return jnp.sum(jnp.where((c % self.size)[..., None] == numbers, places, 0), axis=-1)

        d = (place(jnp.asarray(me)) - place(owner)) % self.size
        return jnp.where(d == 0, 0, jnp.where(d <= self.size // 2, 2 * d - 1, 2 * (self.size - d)))

    def gather(self, block):
        up = down = block
        got = [block]
        for step in range(self.size // 2 - 1):
            up = lax.ppermute(up, "ctx", self.forth)
            down = lax.ppermute(down, "ctx", self.back)
            got += [up, down]
        middle = block.shape[-1] // 2
        up = lax.ppermute(up[..., :middle], "ctx", self.forth)
        down = lax.ppermute(down[..., middle:], "ctx", self.back)
        return got + [jnp.concatenate([up, down], axis=-1)]

    def sum(self, parts):
        middle = parts[0].shape[-1] // 2
        far = parts[self.size - 1]
        up = lax.ppermute(far[..., :middle], "ctx", self.back)
        down = lax.ppermute(far[..., middle:], "ctx", self.forth)
        for step in reversed(range(self.size // 2 - 1)):
            mine_up, mine_down = parts[1 + 2 * step], parts[2 + 2 * step]
            if step == self.size // 2 - 2:
                up = jnp.concatenate([add(mine_up[..., :middle], up), mine_up[..., middle:]], axis=-1)
                down = jnp.concatenate([mine_down[..., :middle], add(mine_down[..., middle:], down)], axis=-1)
            else:
                up, down = add(mine_up, up), add(mine_down, down)
            up = lax.ppermute(up, "ctx", self.back)
            down = lax.ppermute(down, "ctx", self.forth)
        return add(parts[0], up, down)


def add(*terms):
    return sum(x.astype(f32) for x in terms).astype(bf16)


def local(queries, keys, values, out_grad, segment_tiles, parent_list):
    rows_here, key_width = keys.shape
    ctx, heads_axis = lax.axis_size("ctx"), lax.axis_size("head")
    groups = key_width // HD // heads_axis
    heads = queries.shape[1] // key_width
    tiles = ctx * heads_axis * rows_here // TILE
    here = tiles // ctx

    me = lax.axis_index("ctx")
    y_size = heads_axis // 2
    whole = Ring(ctx, ctx, y_size)
    half = Ring(ctx, ctx // 2, y_size)
    partner = [(c, (c + ctx // 2) % ctx) for c in range(ctx)]
    block = jnp.arange(tiles, dtype=jnp.int32) // here
    within = jnp.arange(tiles, dtype=jnp.int32) % here
    slot_of = whole.piece(me, block) * here + within
    other = block // (ctx // 2) != me // (ctx // 2)
    seen_from = jnp.where(other, (me + ctx // 2) % ctx, me)
    half_slot_of = (half.piece(seen_from, block) + jnp.where(other, ctx // 2, 0)) * here + within
    numbers, cnt = visible_lists(segment_tiles, parent_list, me * here, here, tiles)
    slots, half_slots = [renamed(numbers, table) for table in (slot_of, half_slot_of)]

    def swap(x):
        return lax.all_to_all(x, "head", split_axis=0, concat_axis=0, tiled=True)

    def columns(x, number, width):
        return x[:, number * width : (number + 1) * width]

    parts = parts_of(tiles)
    width = heads * HD // parts

    def pair_of_rows(g):
        return jnp.stack(
            [
                jnp.concatenate(
                    [columns(x, (h * groups + g) * parts + p, width) for p in range(parts) for x in (queries, out_grad)],
                    axis=1,
                )
                for h in range(heads_axis)
            ]
        )

    def joined(pieces, which):
        w = pieces[0].shape[2] // (2 * parts)
        return jnp.concatenate(
            [
                columns(pieces[g][h], 2 * p + which, w)
                for h in range(heads_axis)
                for g in range(groups)
                for p in range(parts)
            ],
            axis=1,
        )

    kv = jnp.stack(
        [
            jnp.concatenate([columns(x, h * groups + g, HD) for g in range(groups) for x in (keys, values)], axis=1)
            for h in range(heads_axis)
        ]
    )
    qdo = [pair_of_rows(g) for g in range(groups)]
    kv = swap(kv).reshape(here, TILE, groups * 2 * HD)
    crossed = []
    for g in range(groups):
        if g:
            qdo[g], crossed[g - 1] = lax.optimization_barrier((qdo[g], crossed[g - 1]))
        crossed.append(swap(qdo[g]).reshape(here, TILE, -1))

    odq, dkv = [], []
    for g in range(groups):
        mine = kv[:, :, g * 2 * HD : (g + 1) * 2 * HD]
        if g == 0:
            ring = whole.gather(mine)
            around, vis = jnp.concatenate(ring, axis=0), slots
        else:
            mine, ring[-1] = lax.optimization_barrier((mine, ring[-1]))
            around, vis = lax.all_gather(mine, "ctx", axis=0, tiled=True), numbers
        last = g == groups - 1
        odq_g, dkv_g = attend(vis, slots if last else half_slots, cnt, crossed[g], around, g)
        if g:
            far, odq[g - 1], odq_g, dkv_g = lax.optimization_barrier((far, odq[g - 1], odq_g, dkv_g))
            dkv[g - 1] = half.sum(
                [add(near[i * here : (i + 1) * here], far[i * here : (i + 1) * here]) for i in range(ctx // 2)]
            )
        if last:
            dkv_g = whole.sum([dkv_g[i * here : (i + 1) * here] for i in range(ctx)])
        else:
            near, far = dkv_g[: tiles // 2], lax.ppermute(dkv_g[tiles // 2 :], "ctx", partner)
        odq.append(swap(odq_g.reshape(heads_axis, rows_here, -1)))
        dkv.append(dkv_g)
    dkv[-1], odq[-1] = lax.optimization_barrier((dkv[-1], odq[-1]))
    dkv = swap(jnp.concatenate(dkv, axis=-1).reshape(heads_axis, rows_here, -1))
    dk, dv = [
        jnp.concatenate(
            [columns(dkv[h], 2 * g + which, HD) for h in range(heads_axis) for g in range(groups)], axis=1
        )
        for which in range(2)
    ]
    return joined(odq, 0), joined(odq, 1), dk, dv


def solution(mesh):
    rows = P(("ctx", "head"), None)
    return jax.shard_map(
        local,
        mesh=mesh,
        in_specs=(rows, rows, rows, rows, P(), P()),
        out_specs=(rows, rows, rows, rows),
        check_vma=False,
    )
```

```python
import functools
import math

import jax
import jax.numpy as jnp
from jax import lax
from jax.experimental import pallas as pl
from jax.experimental.pallas import tpu as pltpu
from jax.sharding import PartitionSpec as P

HD = 128
TILE = 128
LEVELS = 4
MOST = 8
WIDE = 8
HALF = WIDE // 2
NEG = -1e30
SCALE = 1.0 / math.sqrt(HD)
LOG2E = 1.4426950408889634
bf16 = jnp.bfloat16
f32 = jnp.float32


def visible_lists(segment_tiles, parent_list, first, here, tiles):
    count = segment_tiles.shape[0]
    ends = jnp.cumsum(segment_tiles, dtype=jnp.int32)
    numbers = jnp.arange(count, dtype=jnp.int32)
    key_tiles = jnp.arange(tiles, dtype=jnp.int32)
    key_seg = jnp.sum((key_tiles[:, None] >= ends[None, :]).astype(jnp.int32), axis=1)
    mine = first + jnp.arange(here, dtype=jnp.int32)
    seg = jnp.sum((mine[:, None] >= ends[None, :]).astype(jnp.int32), axis=1)
    seen = jnp.zeros((here, tiles), jnp.bool_)
    for level in range(LEVELS):
        seen = seen | (seg[:, None] == key_seg[None, :])
        seg = jnp.sum(jnp.where(seg[:, None] == numbers[None, :], parent_list[None, :], 0), axis=1)
    seen = seen & (key_tiles[None, :] <= mine[:, None])
    rank = jnp.cumsum(seen.astype(jnp.int32), axis=1) - 1
    most = min(tiles, LEVELS * MOST)
    places = jnp.arange(most, dtype=jnp.int32)
    chosen = seen[:, :, None] & (rank[:, :, None] == places[None, None, :])
    numbers = jnp.sum(jnp.where(chosen, key_tiles[None, :, None], 0), axis=1)
    return numbers, jnp.sum(seen.astype(jnp.int32), axis=1)


def renamed(numbers, table):
    places = jnp.arange(table.shape[0], dtype=jnp.int32)
    return jnp.sum(jnp.where(numbers[:, :, None] == places, table, 0), axis=2)


def mm(a, b, ca=1, cb=0):
    return lax.dot_general(a, b, (((ca,), (cb,)), ((), ())), preferred_element_type=f32)


def attend_kernel(
    vis, into, cnt, qdo, k, v, odq, near, far, qt, dt, qn, dn, s_buf, p_buf, o_acc, q_acc, dka, dva, *, heads, last
):
    t = pl.program_id(0)
    part = pl.program_id(1)
    rows = heads * TILE

    @pl.when((t == 0) & (part == 0))
    def _():
        dka[...] = jnp.zeros_like(dka)
        dva[...] = jnp.zeros_like(dva)

    for h in range(heads):
        cols = slice(h * HD, (h + 1) * HD)
        qt[:, cols] = qdo[0, :, cols].T
        dt[:, cols] = qdo[0, :, rows + h * HD : rows + (h + 1) * HD].T
        qn[cols, :] = qdo[0, :, cols]
    n = cnt[t]
    wides = (n - 1) // WIDE
    halves = (n - 1) // HALF
    rest = n - halves * HALF

    def gathered(ref, at, wide):
        return jnp.concatenate([ref[vis[t, at + w]] for w in range(wide)], axis=0)

    def rows_of(at, wide):
        return pl.ds(pl.multiple_of(at * TILE, TILE), wide * TILE)

    def over_blocks(step, carry):
        carry = lax.fori_loop(0, wides, lambda b, c: step(b * WIDE, WIDE, False, c), carry)
        carry = lax.cond(
            halves > 2 * wides, lambda c: step(wides * WIDE, HALF, False, c), lambda c: c, carry
        )
        return lax.cond(
            rest <= HALF // 2,
            lambda c: step(halves * HALF, HALF // 2, True, c),
            lambda c: step(halves * HALF, HALF, True, c),
            carry,
        )

    def scores(at, wide, masked, m8):
        s = mm(gathered(k, at, wide), qt[...])
        if masked:
            key = lax.broadcasted_iota(jnp.int32, (wide * TILE, rows), 0)
            token = lax.broadcasted_iota(jnp.int32, (wide * TILE, rows), 1) % TILE
            s = jnp.where(key <= token + (rest - 1) * TILE, s, NEG)
        s_buf[rows_of(at, wide)] = s
        return jnp.maximum(m8, jnp.max(s.reshape(wide * TILE // 8, 8, rows), axis=0))

    m8 = over_blocks(scores, jnp.full((8, rows), NEG, f32))
    m = jnp.max(m8, axis=0, keepdims=True)

    o_acc[...] = jnp.zeros_like(o_acc)

    def weigh(at, wide, masked, l8):
        vb = gathered(v, at, wide)
        p = jnp.exp2((s_buf[rows_of(at, wide)] - m) * (SCALE * LOG2E))
        dp = mm(vb, dt[...])
        pb = p.astype(bf16)
        p_buf[rows_of(at, wide)] = pb
        s_buf[rows_of(at, wide)] = dp
        o_acc[...] += mm(vb, pb, 0, 0)
        return l8 + jnp.sum(p.reshape(wide * TILE // 8, 8, rows), axis=0)

    l8 = over_blocks(weigh, jnp.zeros((8, rows), f32))
    inv = 1.0 / jnp.sum(l8, axis=0, keepdims=True)
    ob = (o_acc[...] * inv).astype(bf16)
    grads = dt[...].astype(f32)
    db = (grads * inv).astype(bf16)
    rowdot = jnp.sum(grads * ob.astype(f32), axis=0, keepdims=True) * inv
    for h in range(heads):
        cols = slice(h * HD, (h + 1) * HD)
        odq[0, :, cols] = ob[:, cols].T
        dn[cols, :] = db[:, cols].T

    q_acc[...] = jnp.zeros_like(q_acc)

    def back(at, wide, masked, carry):
        pb = p_buf[rows_of(at, wide)]
        dp = s_buf[rows_of(at, wide)]
        ds = (pb.astype(f32) * (dp * inv - rowdot)).astype(bf16)
        dvn = mm(pb, dn[...])
        dkn = mm(ds, qn[...])
        q_acc[...] += mm(gathered(k, at, wide), ds, 0, 0)
        for w in range(wide):
            slot = into[t, at + w]
            part_rows = slice(w * TILE, (w + 1) * TILE)
            dva[slot] += dvn[part_rows]
            dka[slot] += dkn[part_rows]
        return carry

    over_blocks(back, 0)
    qb = (q_acc[...] * SCALE).astype(bf16)
    for h in range(heads):
        odq[0, :, rows + h * HD : rows + (h + 1) * HD] = qb[:, h * HD : (h + 1) * HD].T

    @pl.when((t == last[0]) & (part == last[1]))
    def _():
        for at, ref in ((0, near), (near.shape[0], far)):
            own = pl.ds(at, near.shape[0])
            ref[:, :, :HD] = (dka[own] * SCALE).astype(bf16)
            ref[:, :, HD:] = dva[own].astype(bf16)


def parts_of(tiles):
    return 1 if tiles <= 64 else 2


def attend(vis, into, cnt, qdo, kv, number):
    here, _, width = qdo.shape
    tiles = kv.shape[0]
    most = vis.shape[1]
    parts = parts_of(tiles)
    rows = width // (2 * parts)
    rowspec = pl.BlockSpec((1, TILE, 2 * rows), lambda t, p, *_: (t, 0, p))
    keyspec = pl.BlockSpec((tiles, TILE, HD), lambda t, p, *_: (0, 0, 0), pipeline_mode=pl.Buffered(1))
    valspec = pl.BlockSpec((tiles, TILE, HD), lambda t, p, *_: (0, 0, 1), pipeline_mode=pl.Buffered(1))
    gradspec = pl.BlockSpec((tiles // 2, TILE, 2 * HD), lambda t, p, *_: (0, 0, 0), pipeline_mode=pl.Buffered(1))
    return pl.pallas_call(
        functools.partial(attend_kernel, heads=rows // HD, last=(here - 1, parts - 1)),
        grid_spec=pltpu.PrefetchScalarGridSpec(
            num_scalar_prefetch=3,
            grid=(here, parts),
            in_specs=[rowspec, keyspec, valspec],
            out_specs=[rowspec, gradspec, gradspec],
            scratch_shapes=[
                pltpu.VMEM((HD, rows), bf16),
                pltpu.VMEM((HD, rows), bf16),
                pltpu.VMEM((rows, HD), bf16),
                pltpu.VMEM((rows, HD), bf16),
                pltpu.VMEM((most * TILE, rows), f32),
                pltpu.VMEM((most * TILE, rows), bf16),
                pltpu.VMEM((HD, rows), f32),
                pltpu.VMEM((HD, rows), f32),
                pltpu.VMEM((tiles, TILE, HD), f32),
                pltpu.VMEM((tiles, TILE, HD), f32),
            ],
        ),
        out_shape=[
            jax.ShapeDtypeStruct((here, TILE, width), bf16),
            jax.ShapeDtypeStruct((tiles // 2, TILE, 2 * HD), bf16),
            jax.ShapeDtypeStruct((tiles // 2, TILE, 2 * HD), bf16),
        ],
        compiler_params=pltpu.CompilerParams(vmem_limit_bytes=63 << 20),
        cost_estimate=pl.CostEstimate(flops=40_000_000_000, bytes_accessed=20_000_000, transcendentals=20_000_000),
        name=f"attend{number}",
    )(vis, into, cnt, qdo, kv, kv)


def snake(z_size, y_size):
    order = [z * y_size for z in range(z_size)]
    for z in reversed(range(z_size)):
        across = range(1, y_size)
        order += [z * y_size + y for y in (across if (z_size - 1 - z) % 2 == 0 else reversed(across))]
    return order


def pack_kernel(*refs):
    out = refs[-1]
    width = refs[0].shape[1]
    for i, ref in enumerate(refs[:-1]):
        out[0, :, i * width : (i + 1) * width] = ref[...]


def packed(one, two, width, heads_axis, pieces, at, name):
    rows = one.shape[0]
    stride = one.shape[1] // (width * heads_axis)

    def spec(piece):
        return pl.BlockSpec((rows, width), lambda h: (0, h * stride + at + piece))

    return pl.pallas_call(
        pack_kernel,
        grid=(heads_axis,),
        in_specs=[spec(p) for p in range(pieces) for _ in range(2)],
        out_specs=pl.BlockSpec((1, rows, 2 * pieces * width), lambda h: (h, 0, 0)),
        out_shape=jax.ShapeDtypeStruct((heads_axis, rows, 2 * pieces * width), one.dtype),
        cost_estimate=pl.CostEstimate(
            flops=0, bytes_accessed=8 * heads_axis * rows * pieces * width, transcendentals=0
        ),
        name=name,
    )(*[x for _ in range(pieces) for x in (one, two)])


class Ring:
    def __init__(self, ctx, size, y_size):
        order = snake(size // y_size, y_size)
        self.size = size
        self.place = [order.index(c) for c in range(size)]
        self.forth = [
            (at + order[i], at + order[(i + 1) % size]) for at in range(0, ctx, size) for i in range(size)
        ]
        self.back = [(b, a) for a, b in self.forth]

    def piece(self, me, owner):
        places = jnp.asarray(self.place, jnp.int32)
        numbers = jnp.arange(self.size, dtype=jnp.int32)

        def place(c):
            return jnp.sum(jnp.where((c % self.size)[..., None] == numbers, places, 0), axis=-1)

        d = (place(jnp.asarray(me)) - place(owner)) % self.size
        return jnp.where(d == 0, 0, jnp.where(d <= self.size // 2, 2 * d - 1, 2 * (self.size - d)))

    def gather(self, block):
        up = down = block
        got = [block]
        for step in range(self.size // 2 - 1):
            up = lax.ppermute(up, "ctx", self.forth)
            down = lax.ppermute(down, "ctx", self.back)
            got += [up, down]
        middle = block.shape[-1] // 2
        up = lax.ppermute(up[..., :middle], "ctx", self.forth)
        down = lax.ppermute(down[..., middle:], "ctx", self.back)
        return got + [jnp.concatenate([up, down], axis=-1)]

    def sum(self, parts):
        middle = parts[0].shape[-1] // 2
        far = parts[self.size - 1]
        up = lax.ppermute(far[..., :middle], "ctx", self.back)
        down = lax.ppermute(far[..., middle:], "ctx", self.forth)
        for step in reversed(range(self.size // 2 - 1)):
            mine_up, mine_down = parts[1 + 2 * step], parts[2 + 2 * step]
            if step == self.size // 2 - 2:
                up = jnp.concatenate([add(mine_up[..., :middle], up), mine_up[..., middle:]], axis=-1)
                down = jnp.concatenate([mine_down[..., :middle], add(mine_down[..., middle:], down)], axis=-1)
            else:
                up, down = add(mine_up, up), add(mine_down, down)
            up = lax.ppermute(up, "ctx", self.back)
            down = lax.ppermute(down, "ctx", self.forth)
        return add(parts[0], up, down)


def add(*terms):
    return sum(x.astype(f32) for x in terms).astype(bf16)


def local(queries, keys, values, out_grad, segment_tiles, parent_list):
    rows_here, key_width = keys.shape
    ctx, heads_axis = lax.axis_size("ctx"), lax.axis_size("head")
    groups = key_width // HD // heads_axis
    heads = queries.shape[1] // key_width
    tiles = ctx * heads_axis * rows_here // TILE
    here = tiles // ctx

    def swap(x):
        return lax.all_to_all(x, "head", split_axis=0, concat_axis=0, tiled=True)

    def columns(x, number, width):
        return x[:, number * width : (number + 1) * width]

    kv = packed(keys, values, HD, heads_axis, groups, 0, "pack_keys")
    kv = swap(kv).reshape(here, TILE, groups * 2 * HD)
    first = queries, out_grad
    kv, queries, out_grad, segment_tiles, parent_list = lax.optimization_barrier(
        (kv, queries, out_grad, segment_tiles, parent_list)
    )

    me = lax.axis_index("ctx")
    y_size = heads_axis // 2
    whole = Ring(ctx, ctx, y_size)
    half = Ring(ctx, ctx // 2, y_size)
    partner = [(c, (c + ctx // 2) % ctx) for c in range(ctx)]
    block = jnp.arange(tiles, dtype=jnp.int32) // here
    within = jnp.arange(tiles, dtype=jnp.int32) % here
    slot_of = whole.piece(me, block) * here + within
    other = block // (ctx // 2) != me // (ctx // 2)
    seen_from = jnp.where(other, (me + ctx // 2) % ctx, me)
    half_slot_of = (half.piece(seen_from, block) + jnp.where(other, ctx // 2, 0)) * here + within
    numbers, cnt = visible_lists(segment_tiles, parent_list, me * here, here, tiles)
    slots, half_slots = [renamed(numbers, table) for table in (slot_of, half_slot_of)]

    parts = parts_of(tiles)
    width = heads * HD // parts

    def pair_of_rows(g, queries, out_grad):
        return packed(queries, out_grad, width, heads_axis, parts, g * parts, f"pack_rows{g}")

    def joined(pieces, which):
        w = pieces[0].shape[2] // (2 * parts)
        return jnp.concatenate(
            [
                columns(pieces[g][h], 2 * p + which, w)
                for h in range(heads_axis)
                for g in range(groups)
                for p in range(parts)
            ],
            axis=1,
        )

    qdo = [pair_of_rows(g, *((queries, out_grad) if g else first)) for g in range(groups)]
    crossed = []
    for g in range(groups):
        if g:
            qdo[g], crossed[g - 1] = lax.optimization_barrier((qdo[g], crossed[g - 1]))
        crossed.append(swap(qdo[g]).reshape(here, TILE, -1))

    def blocks(x):
        return [x[i * here : (i + 1) * here] for i in range(x.shape[0] // here)]

    odq, dkv = [], []
    for g in range(groups):
        mine = kv[:, :, g * 2 * HD : (g + 1) * 2 * HD]
        if g == 0:
            ring = whole.gather(mine)
            around, vis = jnp.concatenate(ring, axis=0), slots
        else:
            mine, ring[-1] = lax.optimization_barrier((mine, ring[-1]))
            around, vis = lax.all_gather(mine, "ctx", axis=0, tiled=True), numbers
        last = g == groups - 1
        odq_g, near_g, far_g = attend(vis, slots if last else half_slots, cnt, crossed[g], around, g)
        if g:
            far, odq[g - 1], odq_g, near_g, far_g = lax.optimization_barrier((far, odq[g - 1], odq_g, near_g, far_g))
            dkv[g - 1] = half.sum([add(a, b) for a, b in zip(blocks(near), blocks(far))])
        if last:
            dkv_g = whole.sum(blocks(near_g) + blocks(far_g))
        else:
            dkv_g, near, far = None, near_g, lax.ppermute(far_g, "ctx", partner)
        odq.append(swap(odq_g.reshape(heads_axis, rows_here, -1)))
        dkv.append(dkv_g)
    dkv[-1], odq = lax.optimization_barrier((dkv[-1], odq))
    dkv = swap(jnp.concatenate(dkv, axis=-1).reshape(heads_axis, rows_here, -1))
    dk, dv = [
        jnp.concatenate(
            [columns(dkv[h], 2 * g + which, HD) for h in range(heads_axis) for g in range(groups)], axis=1
        )
        for which in range(2)
    ]
    return joined(odq, 0), joined(odq, 1), dk, dv


def solution(mesh):
    rows = P(("ctx", "head"), None)
    return jax.shard_map(
        local,
        mesh=mesh,
        in_specs=(rows, rows, rows, rows, P(), P()),
        out_specs=(rows, rows, rows, rows),
        check_vma=False,
    )
```

```python
import functools
import math

import jax
import jax.numpy as jnp
from jax import lax
from jax.experimental import pallas as pl
from jax.experimental.pallas import tpu as pltpu
from jax.sharding import PartitionSpec as P

HD = 128
TILE = 128
LEVELS = 4
MOST = 8
WIDE = 8
HALF = WIDE // 2
NEG = -1e30
SCALE = 1.0 / math.sqrt(HD)
LOG2E = 1.4426950408889634
bf16 = jnp.bfloat16
f32 = jnp.float32


def visible_lists(segment_tiles, parent_list, first, here, tiles):
    count = segment_tiles.shape[0]
    ends = jnp.cumsum(segment_tiles, dtype=jnp.int32)
    numbers = jnp.arange(count, dtype=jnp.int32)
    key_tiles = jnp.arange(tiles, dtype=jnp.int32)
    key_seg = jnp.sum((key_tiles[:, None] >= ends[None, :]).astype(jnp.int32), axis=1)
    mine = first + jnp.arange(here, dtype=jnp.int32)
    seg = jnp.sum((mine[:, None] >= ends[None, :]).astype(jnp.int32), axis=1)
    seen = jnp.zeros((here, tiles), jnp.bool_)
    for level in range(LEVELS):
        seen = seen | (seg[:, None] == key_seg[None, :])
        seg = jnp.sum(jnp.where(seg[:, None] == numbers[None, :], parent_list[None, :], 0), axis=1)
    seen = seen & (key_tiles[None, :] <= mine[:, None])
    rank = jnp.cumsum(seen.astype(jnp.int32), axis=1) - 1
    most = min(tiles, LEVELS * MOST)
    places = jnp.arange(most, dtype=jnp.int32)
    chosen = seen[:, :, None] & (rank[:, :, None] == places[None, None, :])
    numbers = jnp.sum(jnp.where(chosen, key_tiles[None, :, None], 0), axis=1)
    return numbers, jnp.sum(seen.astype(jnp.int32), axis=1)


def renamed(numbers, table):
    places = jnp.arange(table.shape[0], dtype=jnp.int32)
    return jnp.sum(jnp.where(numbers[:, :, None] == places, table, 0), axis=2)


def mm(a, b, ca=1, cb=0):
    return lax.dot_general(a, b, (((ca,), (cb,)), ((), ())), preferred_element_type=f32)


def attend_kernel(
    vis, into, cnt, qdo, k, v, odq, near, far, qt, dt, qn, dn, s_buf, p_buf, o_acc, q_acc, dka, dva, *, heads, last
):
    t = pl.program_id(0)
    part = pl.program_id(1)
    rows = heads * TILE

    @pl.when((t == 0) & (part == 0))
    def _():
        dka[...] = jnp.zeros_like(dka)
        dva[...] = jnp.zeros_like(dva)

    for h in range(heads):
        cols = slice(h * HD, (h + 1) * HD)
        qt[:, cols] = qdo[0, :, cols].T
        dt[:, cols] = qdo[0, :, rows + h * HD : rows + (h + 1) * HD].T
        qn[cols, :] = qdo[0, :, cols]
    n = cnt[t]
    wides = (n - 1) // WIDE
    halves = (n - 1) // HALF
    rest = n - halves * HALF

    def gathered(ref, at, wide):
        return jnp.concatenate([ref[vis[t, at + w]] for w in range(wide)], axis=0)

    def rows_of(at, wide):
        return pl.ds(pl.multiple_of(at * TILE, TILE), wide * TILE)

    def over_blocks(step, carry):
        carry = lax.fori_loop(0, wides, lambda b, c: step(b * WIDE, WIDE, False, c), carry)
        carry = lax.cond(
            halves > 2 * wides, lambda c: step(wides * WIDE, HALF, False, c), lambda c: c, carry
        )
        return lax.cond(
            rest <= HALF // 2,
            lambda c: step(halves * HALF, HALF // 2, True, c),
            lambda c: step(halves * HALF, HALF, True, c),
            carry,
        )

    def scores(at, wide, masked, m8):
        s = mm(gathered(k, at, wide), qt[...])
        if masked:
            key = lax.broadcasted_iota(jnp.int32, (wide * TILE, rows), 0)
            token = lax.broadcasted_iota(jnp.int32, (wide * TILE, rows), 1) % TILE
            s = jnp.where(key <= token + (rest - 1) * TILE, s, NEG)
        s_buf[rows_of(at, wide)] = s
        return jnp.maximum(m8, jnp.max(s.reshape(wide * TILE // 8, 8, rows), axis=0))

    m8 = over_blocks(scores, jnp.full((8, rows), NEG, f32))
    m = jnp.max(m8, axis=0, keepdims=True)

    o_acc[...] = jnp.zeros_like(o_acc)

    def weigh(at, wide, masked, l8):
        vb = gathered(v, at, wide)
        p = jnp.exp2((s_buf[rows_of(at, wide)] - m) * (SCALE * LOG2E))
        dp = mm(vb, dt[...])
        pb = p.astype(bf16)
        p_buf[rows_of(at, wide)] = pb
        s_buf[rows_of(at, wide)] = dp
        o_acc[...] += mm(vb, pb, 0, 0)
        return l8 + jnp.sum(p.reshape(wide * TILE // 8, 8, rows), axis=0)

    l8 = over_blocks(weigh, jnp.zeros((8, rows), f32))
    inv = 1.0 / jnp.sum(l8, axis=0, keepdims=True)
    ob = (o_acc[...] * inv).astype(bf16)
    grads = dt[...].astype(f32)
    db = (grads * inv).astype(bf16)
    rowdot = jnp.sum(grads * ob.astype(f32), axis=0, keepdims=True) * inv
    for h in range(heads):
        cols = slice(h * HD, (h + 1) * HD)
        odq[0, :, cols] = ob[:, cols].T
        dn[cols, :] = db[:, cols].T

    q_acc[...] = jnp.zeros_like(q_acc)

    def back(at, wide, masked, carry):
        pb = p_buf[rows_of(at, wide)]
        dp = s_buf[rows_of(at, wide)]
        ds = (pb.astype(f32) * (dp * inv - rowdot)).astype(bf16)
        dvn = mm(pb, dn[...])
        dkn = mm(ds, qn[...])
        q_acc[...] += mm(gathered(k, at, wide), ds, 0, 0)
        for w in range(wide):
            slot = into[t, at + w]
            part_rows = slice(w * TILE, (w + 1) * TILE)
            dva[slot] += dvn[part_rows]
            dka[slot] += dkn[part_rows]
        return carry

    over_blocks(back, 0)
    qb = (q_acc[...] * SCALE).astype(bf16)
    for h in range(heads):
        odq[0, :, rows + h * HD : rows + (h + 1) * HD] = qb[:, h * HD : (h + 1) * HD].T

    @pl.when((t == last[0]) & (part == last[1]))
    def _():
        for at, ref in ((0, near), (near.shape[0], far)):
            own = pl.ds(at, near.shape[0])
            ref[:, :, :HD] = (dka[own] * SCALE).astype(bf16)
            ref[:, :, HD:] = dva[own].astype(bf16)


def parts_of(tiles):
    return 1 if tiles <= 64 else 2


def attend(vis, into, cnt, qdo, kv, number):
    here, _, width = qdo.shape
    tiles = kv.shape[0]
    most = vis.shape[1]
    parts = parts_of(tiles)
    rows = width // (2 * parts)
    rowspec = pl.BlockSpec((1, TILE, 2 * rows), lambda t, p, *_: (t, 0, p))
    keyspec = pl.BlockSpec((tiles, TILE, HD), lambda t, p, *_: (0, 0, 0), pipeline_mode=pl.Buffered(1))
    valspec = pl.BlockSpec((tiles, TILE, HD), lambda t, p, *_: (0, 0, 1), pipeline_mode=pl.Buffered(1))
    gradspec = pl.BlockSpec((tiles // 2, TILE, 2 * HD), lambda t, p, *_: (0, 0, 0), pipeline_mode=pl.Buffered(1))
    return pl.pallas_call(
        functools.partial(attend_kernel, heads=rows // HD, last=(here - 1, parts - 1)),
        grid_spec=pltpu.PrefetchScalarGridSpec(
            num_scalar_prefetch=3,
            grid=(here, parts),
            in_specs=[rowspec, keyspec, valspec],
            out_specs=[rowspec, gradspec, gradspec],
            scratch_shapes=[
                pltpu.VMEM((HD, rows), bf16),
                pltpu.VMEM((HD, rows), bf16),
                pltpu.VMEM((rows, HD), bf16),
                pltpu.VMEM((rows, HD), bf16),
                pltpu.VMEM((most * TILE, rows), f32),
                pltpu.VMEM((most * TILE, rows), bf16),
                pltpu.VMEM((HD, rows), f32),
                pltpu.VMEM((HD, rows), f32),
                pltpu.VMEM((tiles, TILE, HD), f32),
                pltpu.VMEM((tiles, TILE, HD), f32),
            ],
        ),
        out_shape=[
            jax.ShapeDtypeStruct((here, TILE, width), bf16),
            jax.ShapeDtypeStruct((tiles // 2, TILE, 2 * HD), bf16),
            jax.ShapeDtypeStruct((tiles // 2, TILE, 2 * HD), bf16),
        ],
        compiler_params=pltpu.CompilerParams(vmem_limit_bytes=63 << 20),
        cost_estimate=pl.CostEstimate(flops=40_000_000_000, bytes_accessed=20_000_000, transcendentals=20_000_000),
        name=f"attend{number}",
    )(vis, into, cnt, qdo, kv, kv)


def snake(z_size, y_size):
    order = [z * y_size for z in range(z_size)]
    for z in reversed(range(z_size)):
        across = range(1, y_size)
        order += [z * y_size + y for y in (across if (z_size - 1 - z) % 2 == 0 else reversed(across))]
    return order


def pack_kernel(*refs):
    out = refs[-1]
    width = refs[0].shape[1]
    for i, ref in enumerate(refs[:-1]):
        out[0, :, i * width : (i + 1) * width] = ref[...]


def packed(one, two, width, heads_axis, pieces, at, name):
    rows = one.shape[0]
    stride = one.shape[1] // (width * heads_axis)

    def spec(piece):
        return pl.BlockSpec((rows, width), lambda h: (0, h * stride + at + piece))

    return pl.pallas_call(
        pack_kernel,
        grid=(heads_axis,),
        in_specs=[spec(p) for p in range(pieces) for _ in range(2)],
        out_specs=pl.BlockSpec((1, rows, 2 * pieces * width), lambda h: (h, 0, 0)),
        out_shape=jax.ShapeDtypeStruct((heads_axis, rows, 2 * pieces * width), one.dtype),
        cost_estimate=pl.CostEstimate(
            flops=0, bytes_accessed=8 * heads_axis * rows * pieces * width, transcendentals=0
        ),
        name=name,
    )(*[x for _ in range(pieces) for x in (one, two)])


class Ring:
    def __init__(self, ctx, size, y_size):
        order = snake(size // y_size, y_size)
        self.size = size
        self.place = [order.index(c) for c in range(size)]
        self.forth = [
            (at + order[i], at + order[(i + 1) % size]) for at in range(0, ctx, size) for i in range(size)
        ]
        self.back = [(b, a) for a, b in self.forth]

    def piece(self, me, owner):
        places = jnp.asarray(self.place, jnp.int32)
        numbers = jnp.arange(self.size, dtype=jnp.int32)

        def place(c):
            return jnp.sum(jnp.where((c % self.size)[..., None] == numbers, places, 0), axis=-1)

        d = (place(jnp.asarray(me)) - place(owner)) % self.size
        return jnp.where(d == 0, 0, jnp.where(d <= self.size // 2, 2 * d - 1, 2 * (self.size - d)))

    def gather(self, block):
        up = down = block
        got = [block]
        for step in range(self.size // 2 - 1):
            up = lax.ppermute(up, "ctx", self.forth)
            down = lax.ppermute(down, "ctx", self.back)
            got += [up, down]
        middle = block.shape[-1] // 2
        up = lax.ppermute(up[..., :middle], "ctx", self.forth)
        down = lax.ppermute(down[..., middle:], "ctx", self.back)
        return got + [jnp.concatenate([up, down], axis=-1)]

    def sum(self, parts):
        middle = parts[0].shape[-1] // 2
        far = parts[self.size - 1]
        up = lax.ppermute(far[..., :middle], "ctx", self.back)
        down = lax.ppermute(far[..., middle:], "ctx", self.forth)
        for step in reversed(range(self.size // 2 - 1)):
            mine_up, mine_down = parts[1 + 2 * step], parts[2 + 2 * step]
            if step == self.size // 2 - 2:
                up = jnp.concatenate([add(mine_up[..., :middle], up), mine_up[..., middle:]], axis=-1)
                down = jnp.concatenate([mine_down[..., :middle], add(mine_down[..., middle:], down)], axis=-1)
            else:
                up, down = add(mine_up, up), add(mine_down, down)
            up = lax.ppermute(up, "ctx", self.back)
            down = lax.ppermute(down, "ctx", self.forth)
        return add(parts[0], up, down)


def add(*terms):
    return sum(x.astype(f32) for x in terms).astype(bf16)


def local(queries, keys, values, out_grad, segment_tiles, parent_list):
    rows_here, key_width = keys.shape
    ctx, heads_axis = lax.axis_size("ctx"), lax.axis_size("head")
    groups = key_width // HD // heads_axis
    heads = queries.shape[1] // key_width
    tiles = ctx * heads_axis * rows_here // TILE
    here = tiles // ctx

    def swap(x):
        return lax.all_to_all(x, "head", split_axis=0, concat_axis=0, tiled=True)

    def swap_small(x):
        own = lax.axis_index("head")

        def pick(y, number):
            return lax.dynamic_index_in_dim(y, own ^ number, 0, keepdims=False)

        came = [pick(x, 0)]
        for k in range(1, heads_axis):
            came.append(lax.ppermute(pick(x, k), "head", [(h, h ^ k) for h in range(heads_axis)]))
        came = jnp.stack(came)
        return jnp.stack([pick(came, h) for h in range(heads_axis)])

    def columns(x, number, width):
        return x[:, number * width : (number + 1) * width]

    kv = packed(keys, values, HD, heads_axis, groups, 0, "pack_keys")
    kv = swap_small(kv).reshape(here, TILE, groups * 2 * HD)
    first = queries, out_grad
    kv, queries, out_grad, segment_tiles, parent_list = lax.optimization_barrier(
        (kv, queries, out_grad, segment_tiles, parent_list)
    )

    me = lax.axis_index("ctx")
    y_size = heads_axis // 2
    whole = Ring(ctx, ctx, y_size)
    half = Ring(ctx, ctx // 2, y_size)
    partner = [(c, (c + ctx // 2) % ctx) for c in range(ctx)]
    block = jnp.arange(tiles, dtype=jnp.int32) // here
    within = jnp.arange(tiles, dtype=jnp.int32) % here
    slot_of = whole.piece(me, block) * here + within
    other = block // (ctx // 2) != me // (ctx // 2)
    seen_from = jnp.where(other, (me + ctx // 2) % ctx, me)
    half_slot_of = (half.piece(seen_from, block) + jnp.where(other, ctx // 2, 0)) * here + within
    numbers, cnt = visible_lists(segment_tiles, parent_list, me * here, here, tiles)
    slots, half_slots = [renamed(numbers, table) for table in (slot_of, half_slot_of)]

    parts = parts_of(tiles)
    width = heads * HD // parts

    def pair_of_rows(g, queries, out_grad):
        return packed(queries, out_grad, width, heads_axis, parts, g * parts, f"pack_rows{g}")

    def joined(pieces, which):
        w = pieces[0].shape[2] // (2 * parts)
        return jnp.concatenate(
            [
                columns(pieces[g][h], 2 * p + which, w)
                for h in range(heads_axis)
                for g in range(groups)
                for p in range(parts)
            ],
            axis=1,
        )

    qdo = [pair_of_rows(g, *((queries, out_grad) if g else first)) for g in range(groups)]
    crossed = []
    for g in range(groups):
        if g:
            qdo[g], crossed[g - 1] = lax.optimization_barrier((qdo[g], crossed[g - 1]))
        crossed.append(swap(qdo[g]).reshape(here, TILE, -1))

    def blocks(x):
        return [x[i * here : (i + 1) * here] for i in range(x.shape[0] // here)]

    odq, dkv = [], []
    for g in range(groups):
        mine = kv[:, :, g * 2 * HD : (g + 1) * 2 * HD]
        if g == 0:
            ring = whole.gather(mine)
            kv, ring[4] = lax.optimization_barrier((kv, ring[4]))
            around, vis = jnp.concatenate(ring, axis=0), slots
        else:
            around, vis = lax.all_gather(mine, "ctx", axis=0, tiled=True), numbers
        last = g == groups - 1
        odq_g, near_g, far_g = attend(vis, slots if last else half_slots, cnt, crossed[g], around, g)
        if g:
            far, odq[g - 1], odq_g, near_g, far_g = lax.optimization_barrier((far, odq[g - 1], odq_g, near_g, far_g))
            dkv[g - 1] = half.sum([add(a, b) for a, b in zip(blocks(near), blocks(far))])
        if last:
            dkv_g = whole.sum(blocks(near_g) + blocks(far_g))
        else:
            dkv_g, near, far = None, near_g, lax.ppermute(far_g, "ctx", partner)
        odq.append(swap(odq_g.reshape(heads_axis, rows_here, -1)))
        dkv.append(dkv_g)
    dkv[-1], odq = lax.optimization_barrier((dkv[-1], odq))
    dkv = swap_small(jnp.concatenate(dkv, axis=-1).reshape(heads_axis, rows_here, -1))
    dk, dv = [
        jnp.concatenate(
            [columns(dkv[h], 2 * g + which, HD) for h in range(heads_axis) for g in range(groups)], axis=1
        )
        for which in range(2)
    ]
    return joined(odq, 0), joined(odq, 1), dk, dv


def solution(mesh):
    rows = P(("ctx", "head"), None)
    return jax.shard_map(
        local,
        mesh=mesh,
        in_specs=(rows, rows, rows, rows, P(), P()),
        out_specs=(rows, rows, rows, rows),
        check_vma=False,
    )
```

```python
import functools
import math

import jax
import jax.numpy as jnp
from jax import lax
from jax.experimental import pallas as pl
from jax.experimental.pallas import tpu as pltpu
from jax.sharding import PartitionSpec as P

HD = 128
TILE = 128
LEVELS = 4
MOST = 8
WIDE = 16
LEAST = 4
NEG = -1e30
SCALE = 1.0 / math.sqrt(HD)
LOG2E = 1.4426950408889634
bf16 = jnp.bfloat16
f32 = jnp.float32


def visible_lists(segment_tiles, parent_list, first, here, tiles):
    count = segment_tiles.shape[0]
    ends = jnp.cumsum(segment_tiles, dtype=jnp.int32)
    numbers = jnp.arange(count, dtype=jnp.int32)
    key_tiles = jnp.arange(tiles, dtype=jnp.int32)
    key_seg = jnp.sum((key_tiles[:, None] >= ends[None, :]).astype(jnp.int32), axis=1)
    mine = first + jnp.arange(here, dtype=jnp.int32)
    seg = jnp.sum((mine[:, None] >= ends[None, :]).astype(jnp.int32), axis=1)
    seen = jnp.zeros((here, tiles), jnp.bool_)
    for level in range(LEVELS):
        seen = seen | (seg[:, None] == key_seg[None, :])
        seg = jnp.sum(jnp.where(seg[:, None] == numbers[None, :], parent_list[None, :], 0), axis=1)
    seen = seen & (key_tiles[None, :] <= mine[:, None])
    rank = jnp.cumsum(seen.astype(jnp.int32), axis=1) - 1
    most = min(tiles, LEVELS * MOST)
    places = jnp.arange(most, dtype=jnp.int32)
    chosen = seen[:, :, None] & (rank[:, :, None] == places[None, None, :])
    numbers = jnp.sum(jnp.where(chosen, key_tiles[None, :, None], 0), axis=1)
    return numbers, jnp.sum(seen.astype(jnp.int32), axis=1)


def renamed(numbers, table):
    places = jnp.arange(table.shape[0], dtype=jnp.int32)
    return jnp.sum(jnp.where(numbers[:, :, None] == places, table, 0), axis=2)


def mm(a, b, ca=1, cb=0):
    return lax.dot_general(a, b, (((ca,), (cb,)), ((), ())), preferred_element_type=f32)


def attend_kernel(
    vis, into, cnt, qdo, k, v, odq, near, far, qt, dt, qn, dn, s_buf, p_buf, o_acc, q_acc, dka, dva, *, heads, last
):
    t = pl.program_id(0)
    part = pl.program_id(1)
    rows = heads * TILE

    @pl.when((t == 0) & (part == 0))
    def _():
        dka[...] = jnp.zeros_like(dka)
        dva[...] = jnp.zeros_like(dva)

    for h in range(heads):
        cols = slice(h * HD, (h + 1) * HD)
        qt[:, cols] = qdo[0, :, cols].T
        dt[:, cols] = qdo[0, :, rows + h * HD : rows + (h + 1) * HD].T
        qn[cols, :] = qdo[0, :, cols]
    n = cnt[t]
    most = (n - 1) // WIDE
    rest = n - (n - 1) // LEAST * LEAST

    def gathered(ref, at, wide):
        return jnp.concatenate([ref[vis[t, at + w]] for w in range(wide)], axis=0)

    def rows_of(at, wide):
        return pl.ds(pl.multiple_of(at * TILE, TILE), wide * TILE)

    def over_blocks(step, carry):
        carry = lax.fori_loop(0, most, lambda b, c: step(b * WIDE, WIDE, False, c), carry)
        wide = WIDE // 2
        while wide >= LEAST:
            at = (n - 1) // (2 * wide) * (2 * wide)
            carry = lax.cond(
                (n - 1) // wide % 2 == 1, lambda c: step(at, wide, False, c), lambda c: c, carry
            )
            wide = wide // 2
        at = n - rest
        return lax.cond(
            rest <= LEAST // 2,
            lambda c: step(at, LEAST // 2, True, c),
            lambda c: step(at, LEAST, True, c),
            carry,
        )

    def scores(at, wide, masked, m8):
        s = mm(gathered(k, at, wide), qt[...])
        if masked:
            key = lax.broadcasted_iota(jnp.int32, (wide * TILE, rows), 0)
            token = lax.broadcasted_iota(jnp.int32, (wide * TILE, rows), 1) % TILE
            s = jnp.where(key <= token + (rest - 1) * TILE, s, NEG)
        s_buf[rows_of(at, wide)] = s
        return jnp.maximum(m8, jnp.max(s.reshape(wide * TILE // 8, 8, rows), axis=0))

    m8 = over_blocks(scores, jnp.full((8, rows), NEG, f32))
    m = jnp.max(m8, axis=0, keepdims=True)

    o_acc[...] = jnp.zeros_like(o_acc)

    def weigh(at, wide, masked, l8):
        vb = gathered(v, at, wide)
        p = jnp.exp2((s_buf[rows_of(at, wide)] - m) * (SCALE * LOG2E))
        dp = mm(vb, dt[...])
        pb = p.astype(bf16)
        p_buf[rows_of(at, wide)] = pb
        s_buf[rows_of(at, wide)] = dp
        o_acc[...] += mm(vb, pb, 0, 0)
        return l8 + jnp.sum(p.reshape(wide * TILE // 8, 8, rows), axis=0)

    l8 = over_blocks(weigh, jnp.zeros((8, rows), f32))
    inv = 1.0 / jnp.sum(l8, axis=0, keepdims=True)
    ob = (o_acc[...] * inv).astype(bf16)
    grads = dt[...].astype(f32)
    db = (grads * inv).astype(bf16)
    rowdot = jnp.sum(grads * ob.astype(f32), axis=0, keepdims=True) * inv
    for h in range(heads):
        cols = slice(h * HD, (h + 1) * HD)
        odq[0, :, cols] = ob[:, cols].T
        dn[cols, :] = db[:, cols].T

    q_acc[...] = jnp.zeros_like(q_acc)

    def back(at, wide, masked, carry):
        pb = p_buf[rows_of(at, wide)]
        dp = s_buf[rows_of(at, wide)]
        ds = (pb.astype(f32) * (dp * inv - rowdot)).astype(bf16)
        dvn = mm(pb, dn[...])
        dkn = mm(ds, qn[...])
        q_acc[...] += mm(gathered(k, at, wide), ds, 0, 0)
        for w in range(wide):
            slot = into[t, at + w]
            part_rows = slice(w * TILE, (w + 1) * TILE)
            dva[slot] += dvn[part_rows]
            dka[slot] += dkn[part_rows]
        return carry

    over_blocks(back, 0)
    qb = (q_acc[...] * SCALE).astype(bf16)
    for h in range(heads):
        odq[0, :, rows + h * HD : rows + (h + 1) * HD] = qb[:, h * HD : (h + 1) * HD].T

    @pl.when((t == last[0]) & (part == last[1]))
    def _():
        for at, ref in ((0, near), (near.shape[0], far)):
            own = pl.ds(at, near.shape[0])
            ref[:, :, :HD] = (dka[own] * SCALE).astype(bf16)
            ref[:, :, HD:] = dva[own].astype(bf16)


def parts_of(tiles):
    return 1 if tiles <= 64 else 2


def attend(vis, into, cnt, qdo, kv, number):
    here, _, width = qdo.shape
    tiles = kv.shape[0]
    most = vis.shape[1]
    parts = parts_of(tiles)
    rows = width // (2 * parts)
    rowspec = pl.BlockSpec((1, TILE, 2 * rows), lambda t, p, *_: (t, 0, p))
    keyspec = pl.BlockSpec((tiles, TILE, HD), lambda t, p, *_: (0, 0, 0), pipeline_mode=pl.Buffered(1))
    valspec = pl.BlockSpec((tiles, TILE, HD), lambda t, p, *_: (0, 0, 1), pipeline_mode=pl.Buffered(1))
    gradspec = pl.BlockSpec((tiles // 2, TILE, 2 * HD), lambda t, p, *_: (0, 0, 0), pipeline_mode=pl.Buffered(1))
    return pl.pallas_call(
        functools.partial(attend_kernel, heads=rows // HD, last=(here - 1, parts - 1)),
        grid_spec=pltpu.PrefetchScalarGridSpec(
            num_scalar_prefetch=3,
            grid=(here, parts),
            in_specs=[rowspec, keyspec, valspec],
            out_specs=[rowspec, gradspec, gradspec],
            scratch_shapes=[
                pltpu.VMEM((HD, rows), bf16),
                pltpu.VMEM((HD, rows), bf16),
                pltpu.VMEM((rows, HD), bf16),
                pltpu.VMEM((rows, HD), bf16),
                pltpu.VMEM((most * TILE, rows), f32),
                pltpu.VMEM((most * TILE, rows), bf16),
                pltpu.VMEM((HD, rows), f32),
                pltpu.VMEM((HD, rows), f32),
                pltpu.VMEM((tiles, TILE, HD), f32),
                pltpu.VMEM((tiles, TILE, HD), f32),
            ],
        ),
        out_shape=[
            jax.ShapeDtypeStruct((here, TILE, width), bf16),
            jax.ShapeDtypeStruct((tiles // 2, TILE, 2 * HD), bf16),
            jax.ShapeDtypeStruct((tiles // 2, TILE, 2 * HD), bf16),
        ],
        compiler_params=pltpu.CompilerParams(vmem_limit_bytes=63 << 20),
        cost_estimate=pl.CostEstimate(flops=40_000_000_000, bytes_accessed=20_000_000, transcendentals=20_000_000),
        name=f"attend{number}",
    )(vis, into, cnt, qdo, kv, kv)


def snake(z_size, y_size):
    order = [z * y_size for z in range(z_size)]
    for z in reversed(range(z_size)):
        across = range(1, y_size)
        order += [z * y_size + y for y in (across if (z_size - 1 - z) % 2 == 0 else reversed(across))]
    return order


def pack_kernel(*refs):
    out = refs[-1]
    width = refs[0].shape[1]
    for i, ref in enumerate(refs[:-1]):
        out[0, :, i * width : (i + 1) * width] = ref[...]


def packed(one, two, width, heads_axis, pieces, at, name):
    rows = one.shape[0]
    stride = one.shape[1] // (width * heads_axis)

    def spec(piece):
        return pl.BlockSpec((rows, width), lambda h: (0, h * stride + at + piece))

    return pl.pallas_call(
        pack_kernel,
        grid=(heads_axis,),
        in_specs=[spec(p) for p in range(pieces) for _ in range(2)],
        out_specs=pl.BlockSpec((1, rows, 2 * pieces * width), lambda h: (h, 0, 0)),
        out_shape=jax.ShapeDtypeStruct((heads_axis, rows, 2 * pieces * width), one.dtype),
        cost_estimate=pl.CostEstimate(
            flops=0, bytes_accessed=8 * heads_axis * rows * pieces * width, transcendentals=0
        ),
        name=name,
    )(*[x for _ in range(pieces) for x in (one, two)])


class Ring:
    def __init__(self, ctx, size, y_size):
        order = snake(size // y_size, y_size)
        self.size = size
        self.place = [order.index(c) for c in range(size)]
        self.forth = [
            (at + order[i], at + order[(i + 1) % size]) for at in range(0, ctx, size) for i in range(size)
        ]
        self.back = [(b, a) for a, b in self.forth]

    def piece(self, me, owner):
        places = jnp.asarray(self.place, jnp.int32)
        numbers = jnp.arange(self.size, dtype=jnp.int32)

        def place(c):
            return jnp.sum(jnp.where((c % self.size)[..., None] == numbers, places, 0), axis=-1)

        d = (place(jnp.asarray(me)) - place(owner)) % self.size
        return jnp.where(d == 0, 0, jnp.where(d <= self.size // 2, 2 * d - 1, 2 * (self.size - d)))

    def gather(self, block):
        up = down = block
        got = [block]
        for step in range(self.size // 2 - 1):
            up = lax.ppermute(up, "ctx", self.forth)
            down = lax.ppermute(down, "ctx", self.back)
            got += [up, down]
        middle = block.shape[-1] // 2
        up = lax.ppermute(up[..., :middle], "ctx", self.forth)
        down = lax.ppermute(down[..., middle:], "ctx", self.back)
        return got + [jnp.concatenate([up, down], axis=-1)]

    def sum(self, parts):
        middle = parts[0].shape[-1] // 2
        far = parts[self.size - 1]
        up = lax.ppermute(far[..., :middle], "ctx", self.back)
        down = lax.ppermute(far[..., middle:], "ctx", self.forth)
        for step in reversed(range(self.size // 2 - 1)):
            mine_up, mine_down = parts[1 + 2 * step], parts[2 + 2 * step]
            if step == self.size // 2 - 2:
                up = jnp.concatenate([add(mine_up[..., :middle], up), mine_up[..., middle:]], axis=-1)
                down = jnp.concatenate([mine_down[..., :middle], add(mine_down[..., middle:], down)], axis=-1)
            else:
                up, down = add(mine_up, up), add(mine_down, down)
            up = lax.ppermute(up, "ctx", self.back)
            down = lax.ppermute(down, "ctx", self.forth)
        return add(parts[0], up, down)


def add(*terms):
    return sum(x.astype(f32) for x in terms).astype(bf16)


def local(queries, keys, values, out_grad, segment_tiles, parent_list):
    rows_here, key_width = keys.shape
    ctx, heads_axis = lax.axis_size("ctx"), lax.axis_size("head")
    groups = key_width // HD // heads_axis
    heads = queries.shape[1] // key_width
    tiles = ctx * heads_axis * rows_here // TILE
    here = tiles // ctx

    def swap(x):
        return lax.all_to_all(x, "head", split_axis=0, concat_axis=0, tiled=True)

    def swap_small(x):
        own = lax.axis_index("head")

        def pick(y, number):
            return lax.dynamic_index_in_dim(y, own ^ number, 0, keepdims=False)

        came = [pick(x, 0)]
        for k in range(1, heads_axis):
            came.append(lax.ppermute(pick(x, k), "head", [(h, h ^ k) for h in range(heads_axis)]))
        came = jnp.stack(came)
        return jnp.stack([pick(came, h) for h in range(heads_axis)])

    def columns(x, number, width):
        return x[:, number * width : (number + 1) * width]

    kv = packed(keys, values, HD, heads_axis, groups, 0, "pack_keys")
    kv = swap_small(kv).reshape(here, TILE, groups * 2 * HD)
    first = queries, out_grad
    kv, queries, out_grad, segment_tiles, parent_list = lax.optimization_barrier(
        (kv, queries, out_grad, segment_tiles, parent_list)
    )

    me = lax.axis_index("ctx")
    y_size = heads_axis // 2
    whole = Ring(ctx, ctx, y_size)
    half = Ring(ctx, ctx // 2, y_size)
    partner = [(c, (c + ctx // 2) % ctx) for c in range(ctx)]
    block = jnp.arange(tiles, dtype=jnp.int32) // here
    within = jnp.arange(tiles, dtype=jnp.int32) % here
    slot_of = whole.piece(me, block) * here + within
    other = block // (ctx // 2) != me // (ctx // 2)
    seen_from = jnp.where(other, (me + ctx // 2) % ctx, me)
    half_slot_of = (half.piece(seen_from, block) + jnp.where(other, ctx // 2, 0)) * here + within
    numbers, cnt = visible_lists(segment_tiles, parent_list, me * here, here, tiles)
    slots, half_slots = [renamed(numbers, table) for table in (slot_of, half_slot_of)]

    parts = parts_of(tiles)
    width = heads * HD // parts

    def pair_of_rows(g, queries, out_grad):
        return packed(queries, out_grad, width, heads_axis, parts, g * parts, f"pack_rows{g}")

    def joined(pieces, which):
        w = pieces[0].shape[2] // (2 * parts)
        return jnp.concatenate(
            [
                columns(pieces[g][h], 2 * p + which, w)
                for h in range(heads_axis)
                for g in range(groups)
                for p in range(parts)
            ],
            axis=1,
        )

    qdo = [pair_of_rows(g, *((queries, out_grad) if g else first)) for g in range(groups)]
    crossed = []
    for g in range(groups):
        if g:
            qdo[g], crossed[g - 1] = lax.optimization_barrier((qdo[g], crossed[g - 1]))
        crossed.append(swap(qdo[g]).reshape(here, TILE, -1))

    def blocks(x):
        return [x[i * here : (i + 1) * here] for i in range(x.shape[0] // here)]

    odq, dkv = [], []
    for g in range(groups):
        mine = kv[:, :, g * 2 * HD : (g + 1) * 2 * HD]
        if g == 0:
            ring = whole.gather(mine)
            kv, ring[4] = lax.optimization_barrier((kv, ring[4]))
            around, vis = jnp.concatenate(ring, axis=0), slots
        else:
            around, vis = lax.all_gather(mine, "ctx", axis=0, tiled=True), numbers
        last = g == groups - 1
        odq_g, near_g, far_g = attend(vis, slots if last else half_slots, cnt, crossed[g], around, g)
        if g:
            far, odq[g - 1], odq_g, near_g, far_g = lax.optimization_barrier((far, odq[g - 1], odq_g, near_g, far_g))
            dkv[g - 1] = half.sum([add(a, b) for a, b in zip(blocks(near), blocks(far))])
        if last:
            dkv_g = whole.sum(blocks(near_g) + blocks(far_g))
        else:
            dkv_g, near, far = None, near_g, lax.ppermute(far_g, "ctx", partner)
        odq.append(swap(odq_g.reshape(heads_axis, rows_here, -1)))
        dkv.append(dkv_g)
    dkv[-1], odq = lax.optimization_barrier((dkv[-1], odq))
    dkv = swap_small(jnp.concatenate(dkv, axis=-1).reshape(heads_axis, rows_here, -1))
    dk, dv = [
        jnp.concatenate(
            [columns(dkv[h], 2 * g + which, HD) for h in range(heads_axis) for g in range(groups)], axis=1
        )
        for which in range(2)
    ]
    return joined(odq, 0), joined(odq, 1), dk, dv


def solution(mesh):
    rows = P(("ctx", "head"), None)
    return jax.shard_map(
        local,
        mesh=mesh,
        in_specs=(rows, rows, rows, rows, P(), P()),
        out_specs=(rows, rows, rows, rows),
        check_vma=False,
    )
```
